32 devices in a mesh: occ: 8 (over y, x, core), virt: 4 (over z).
Axes of the slice: x: 2, y: 2, z: 4, core: 2. Of those that a mesh axis runs over, the one named last changes fastest.
Arguments:
- amplitudes: bfloat16 [4096, 1024], P('occ'), may hold values from -6 to 6
- amp_map: int32 [64, 8], P('occ'), may hold values 0 or 1
- integrals: bfloat16 [1024, 1024], P('occ', 'virt'), may hold values from -0.1875 to 0.1875
- int_map: int32 [8, 8], P(None, 'virt'), may hold values 0 or 1
- exchange: bfloat16 [4096, 1024], P('occ', 'virt'), may hold values from -0.1875 to 0.1875
- residual_in: float32 [4096, 1024], P('occ', 'virt'), may hold values from -6 to 6
Outputs:
- residual: float32 [4096, 1024], P('occ', 'virt')
- pair_energy: float32 [4096], P('occ')
The draws below stay inside these ranges and needn't reach their ends.
All inputs are finite; a program needn't handle non-finite values. No bound on the sum of `amp_map` or of `int_map` on one device may be relied on, other than what follows from the above.
Results may differ from the reference program's by a relative error of at most 0.0003.
Values may be sent and summed in bfloat16 or wider, within the bound.
A program may use at most 64 MiB of HBM per device.

```python
import jax
import jax.numpy as jnp
from jax import lax

PTILE = 64
VTILE = 128
PT = 64
KT = 8
PAIRS = 4096
K = 1024


def set_ends(drawn, stream_key, least, top_value):
    longest = drawn.shape.index(max(drawn.shape))
    spots = []
    for shift in (0, 1):
        where = [jax.random.randint(jax.random.fold_in(stream_key, axis), (), 0, length) for axis, length in enumerate(drawn.shape)]
        where[longest] = (where[longest] + shift) % drawn.shape[longest]
        spots.append(tuple(where))
    return drawn.at[spots[0]].set(least).at[spots[1]].set(top_value)


def block_levels(rng, extent, cuts, low, top_value):
    def one(position, shards_of):
        steps = jax.random.uniform(jax.random.fold_in(jax.random.fold_in(rng, 6), position), (shards_of,), jnp.float32, low / len(cuts), top_value / len(cuts))
        return jnp.repeat(jnp.exp(steps), extent[position] // shards_of).reshape((-1,) + (1,) * (len(extent) - position - 1))

    loudness = one(*cuts[0])
    for cut in cuts[1:]:
        loudness = loudness * one(*cut)
    return loudness


def scatter_about(own_key, shape, deviation, limit, shards=(), held_as=jnp.bfloat16):
    array = deviation * jax.random.normal(own_key, shape, jnp.float32)
    if shards:
        array = array * block_levels(own_key, shape, shards, -0.22, 0.18)
    return jnp.clip(array, -limit, limit).astype(held_as)


def setup_inputs(seed: int = 0) -> dict:
    seeds = jax.random.split(jax.random.key(seed), 7)
    return {
        "amplitudes": scatter_about(seeds[0], (PAIRS, K), 1.0, 6.0, ((0, 8),)),
        "amp_map": set_ends((jax.random.randint(seeds[1], (PT, KT), 0, 4) < 3).astype(jnp.int32), jax.random.fold_in(seeds[1], 1), 0, 1),
        "integrals": scatter_about(seeds[2], (K, K), K ** -0.5, 0.1875, ((0, 8), (1, 4))),
        "int_map": set_ends((jax.random.randint(seeds[3], (KT, KT), 0, 4) < 3).astype(jnp.int32), jax.random.fold_in(seeds[3], 1), 0, 1),
        "exchange": scatter_about(seeds[4], (PAIRS, K), K ** -0.5, 0.1875, ((0, 8), (1, 4))),
        "residual_in": scatter_about(seeds[5], (PAIRS, K), 1.0, 6.0, ((0, 8), (1, 4)), jnp.float32),
    }


def expand(table, tall, wide):
    return jnp.repeat(jnp.repeat(table, tall, axis=0), wide, axis=1)


def reference(amplitudes, amp_map, integrals, int_map, exchange, residual_in):
    int_masked = integrals.astype(jnp.float32) * expand(int_map, VTILE, VTILE).astype(jnp.float32)
    tiles = amplitudes.reshape(PT, PTILE, KT, VTILE).astype(jnp.float32)
    tiles = tiles * amp_map.astype(jnp.float32)[:, None, :, None]
    amp_masked = tiles.reshape(PT * PTILE, KT * VTILE)
    product = jnp.dot(amp_masked, int_masked, precision=lax.Precision.HIGHEST, preferred_element_type=jnp.float32)
    residual = residual_in + product
    pair_energy = jnp.sum(residual * exchange.astype(jnp.float32), axis=1)
    return residual, pair_energy
```

```python
import functools

import jax
import jax.numpy as jnp
from jax import lax
from jax.experimental import pallas as pl
from jax.experimental.pallas import tpu as pltpu
from jax.sharding import PartitionSpec as P

PTILE = 64
VTILE = 128
LANES = 128
MESH = pl.DeviceIdType.MESH


def flipped(index, bits):
    out, place = 0, 1
    top = 0
    while place <= bits:
        digit = lax.rem(index // place, 2)
        flip = (bits // place) % 2
        out = out + (1 - digit if flip else digit) * place
        place *= 2
        top = place
    return out + (index // top) * top if top else index


def kernel(
    n, nv,
    amp_hbm, amap_hbm, int_hbm, imap_hbm, exch_hbm, res_hbm,
    out_ref, energy_ref,
    amp, amap, panel, imap, exch, acc, slots,
    in_sem, core_send, core_recv, chip_send, chip_recv, en_send, en_recv,
):
    me = lax.axis_index("occ")
    mv = lax.axis_index("virt")
    chips = n // 2
    chip, core = me // 2, lax.rem(me, 2)
    mate = chip * 2 + (1 - core)
    depth = int_hbm.shape[0]
    rows, cols = out_ref.shape

    def block(owner):
        return panel.at[pl.ds(pl.multiple_of(owner * depth, depth), depth), :]

    loads = [
        pltpu.make_async_copy(int_hbm, block(me), in_sem.at[0]),
        pltpu.make_async_copy(imap_hbm, imap, in_sem.at[1]),
        pltpu.make_async_copy(amp_hbm, amp, in_sem.at[2]),
        pltpu.make_async_copy(amap_hbm, amap, in_sem.at[3]),
        pltpu.make_async_copy(res_hbm, acc, in_sem.at[4]),
        pltpu.make_async_copy(exch_hbm, exch, in_sem.at[5]),
    ]
    for load in loads:
        load.start()

    partners = [flipped(chip, s) for s in range(chips)]
    barrier = pltpu.get_barrier_semaphore()
    pl.semaphore_signal(barrier, inc=1, device_id=(mate, mv), device_id_type=MESH)
    for s in range(1, chips):
        pl.semaphore_signal(barrier, inc=1, device_id=(partners[s] * 2 + core, mv), device_id_type=MESH)
    for s in range(1, nv):
        pl.semaphore_signal(barrier, inc=1, device_id=(me, lax.rem(mv + s, nv)), device_id_type=MESH)

    loads[0].wait()
    loads[1].wait()
    grain = min(depth, VTILE)
    while depth % grain or VTILE % grain:
        grain //= 2
    for t in range(depth // grain):
        tile = (me * depth + t * grain) // VTILE
        here = pl.ds(pl.multiple_of(me * depth + t * grain, grain), grain)
        for c in range(cols // VTILE):
            wide = pl.ds(c * VTILE, VTILE)
            keep = imap[c, tile].astype(jnp.float32).astype(jnp.bfloat16)
            panel[here, wide] = panel[here, wide] * keep

    pl.semaphore_wait(barrier, chips + nv - 1)

    def to_mate(s):
        owner = partners[s] * 2 + core
        return pltpu.make_async_remote_copy(
            src_ref=block(owner), dst_ref=block(owner),
            send_sem=core_send.at[s], recv_sem=core_recv.at[s],
            device_id=(mate, mv), device_id_type=MESH,
        )

    def to_chip(s):
        return pltpu.make_async_remote_copy(
            src_ref=block(me), dst_ref=block(me),
            send_sem=chip_send.at[s], recv_sem=chip_recv.at[s],
            device_id=(partners[s] * 2 + core, mv), device_id_type=MESH,
        )

    def from_chip(s):
        owner = partners[s] * 2 + core
        return pltpu.make_async_remote_copy(
            src_ref=block(owner), dst_ref=block(owner),
            send_sem=chip_send.at[s], recv_sem=chip_recv.at[s],
            device_id=(partners[s] * 2 + core, mv), device_id_type=MESH,
        )

    def from_mate(s):
        owner = partners[s] * 2 + (1 - core)
        return pltpu.make_async_remote_copy(
            src_ref=block(owner), dst_ref=block(owner),
            send_sem=core_send.at[s], recv_sem=core_recv.at[s],
            device_id=(mate, mv), device_id_type=MESH,
        )

    chip_copies = [None] + [to_chip(s) for s in range(1, chips)]
    mate_copies = [to_mate(s) for s in range(chips)]
    for s in range(1, chips):
        chip_copies[s].start()
    mate_copies[0].start()

    loads[2].wait()
    loads[3].wait()
    for r in range(rows // PTILE):
        tall = pl.ds(r * PTILE, PTILE)
        for k in range(amp.shape[1] // VTILE):
            wide = pl.ds(k * VTILE, VTILE)
            keep = amap[r, k].astype(jnp.float32).astype(jnp.bfloat16)
            amp[tall, wide] = amp[tall, wide] * keep
    loads[4].wait()
    loads[5].wait()

    def product(s):
        span = 2 * depth
        start = partners[s] * span
        return jnp.dot(
            amp[:, pl.ds(pl.multiple_of(start, LANES), span)],
            panel[pl.ds(pl.multiple_of(start, LANES), span), :],
            preferred_element_type=jnp.float32,
        )

    for s in range(chips):
        if s + 1 < chips:
            if s == 0:
                from_mate(0).wait_recv()
                acc[...] += product(0)
            from_chip(s + 1).wait_recv()
            mate_copies[s + 1].start()
        if s > 0:
            from_mate(s).wait_recv()
            if s < chips - 1:
                acc[...] += product(s)

    residual = acc[...] + product(chips - 1)
    out_ref[...] = residual
    terms = residual * exch[...].astype(jnp.float32)
    folded = terms[:, :LANES]
    for c in range(1, cols // LANES):
        folded = folded + terms[:, c * LANES:(c + 1) * LANES]
    for q in range(rows // LANES):
        part = folded[q * LANES:(q + 1) * LANES, :].T
        slots[mv, pl.ds(q, 1), :] = jnp.sum(part, axis=0, keepdims=True)

    sends = []
    for s in range(1, nv):
        send = pltpu.make_async_remote_copy(
            src_ref=slots.at[mv], dst_ref=slots.at[mv],
            send_sem=en_send.at[s], recv_sem=en_recv.at[s],
            device_id=(me, lax.rem(mv + s, nv)), device_id_type=MESH,
        )
        send.start()
        sends.append(send)
    for s in range(1, nv):
        origin = lax.rem(mv + nv - s, nv)
        pltpu.make_async_remote_copy(
            src_ref=slots.at[origin], dst_ref=slots.at[origin],
            send_sem=en_send.at[s], recv_sem=en_recv.at[s],
            device_id=(me, origin), device_id_type=MESH,
        ).wait_recv()
    total = slots[0]
    for v in range(1, nv):
        total = total + slots[v]
    energy_ref[...] = total

    for send in sends:
        send.wait_send()
    for s in range(1, chips):
        chip_copies[s].wait_send()
    for s in range(chips):
        mate_copies[s].wait_send()


def solution(mesh):
    n, nv = mesh.shape["occ"], mesh.shape["virt"]
    chips = n // 2

    def on_device(amplitudes, amp_map, integrals, int_map, exchange, residual_in):
        rows, k = amplitudes.shape
        depth, cols = integrals.shape
        imap = int_map.T
        held = 2 * rows * k + 2 * k * cols + 2 * rows * cols + 8 * rows * cols
        hbm = pl.BlockSpec(memory_space=pltpu.HBM)
        vmem = pl.BlockSpec(memory_space=pltpu.VMEM)
        residual, energy = pl.pallas_call(
            functools.partial(kernel, n, nv),
            out_shape=(
                jax.ShapeDtypeStruct((rows, cols), jnp.float32),
                jax.ShapeDtypeStruct((rows // LANES, LANES), jnp.float32),
            ),
            in_specs=[hbm] * 6,
            out_specs=(vmem, vmem),
            scratch_shapes=[
                pltpu.VMEM((rows, k), jnp.bfloat16),
                pltpu.SMEM(amp_map.shape, jnp.int32),
                pltpu.VMEM((k, cols), jnp.bfloat16),
                pltpu.SMEM(imap.shape, jnp.int32),
                pltpu.VMEM((rows, cols), jnp.bfloat16),
                pltpu.VMEM((rows, cols), jnp.float32),
                pltpu.VMEM((nv, rows // LANES, LANES), jnp.float32),
                pltpu.SemaphoreType.DMA((6,)),
                pltpu.SemaphoreType.DMA((chips,)),
                pltpu.SemaphoreType.DMA((chips,)),
                pltpu.SemaphoreType.DMA((chips,)),
                pltpu.SemaphoreType.DMA((chips,)),
                pltpu.SemaphoreType.DMA((nv,)),
                pltpu.SemaphoreType.DMA((nv,)),
            ],
            compiler_params=pltpu.CompilerParams(
                collective_id=0, has_side_effects=True, vmem_limit_bytes=held + (8 << 20)
            ),
            cost_estimate=pl.CostEstimate(flops=2 * rows * k * cols, bytes_accessed=held, transcendentals=0),
        )(amplitudes, amp_map, integrals, imap, exchange, residual_in)
        return residual, energy.reshape(rows)

    in_specs = (
        P("occ", None),
        P("occ", None),
        P("occ", "virt"),
        P(None, "virt"),
        P("occ", "virt"),
        P("occ", "virt"),
    )
    out_specs = (P("occ", "virt"), P("occ"))
    return jax.shard_map(on_device, mesh=mesh, in_specs=in_specs, out_specs=out_specs, check_vma=False)
```

```python
import functools

import jax
import jax.numpy as jnp
from jax import lax
from jax.experimental import pallas as pl
from jax.experimental.pallas import tpu as pltpu
from jax.sharding import PartitionSpec as P

PTILE = 64
VTILE = 128
LANES = 128
MESH = pl.DeviceIdType.MESH


def flipped(index, bits):
    out, place = 0, 1
    top = 0
    while place <= bits:
        digit = lax.rem(index // place, 2)
        flip = (bits // place) % 2
        out = out + (1 - digit if flip else digit) * place
        place *= 2
        top = place
    return out + (index // top) * top if top else index


def kernel(
    n, nv,
    amp_hbm, amap_hbm, int_hbm, imap_hbm, exch_hbm, res_hbm,
    out_ref, energy_ref,
    amp, amap, panel, screened, imap, exch, acc, slots,
    in_sem, core_send, core_recv, chip_send, chip_recv, en_send, en_recv,
):
    me = lax.axis_index("occ")
    mv = lax.axis_index("virt")
    chips = n // 2
    chip, core = me // 2, lax.rem(me, 2)
    mate = chip * 2 + (1 - core)
    depth = int_hbm.shape[0]
    rows, cols = out_ref.shape

    def block(owner):
        return panel.at[pl.ds(pl.multiple_of(owner * depth, depth), depth), :]

    loads = [
        pltpu.make_async_copy(int_hbm, block(me), in_sem.at[0]),
        pltpu.make_async_copy(imap_hbm, imap, in_sem.at[1]),
        pltpu.make_async_copy(amp_hbm, amp, in_sem.at[2]),
        pltpu.make_async_copy(amap_hbm, amap, in_sem.at[3]),
        pltpu.make_async_copy(res_hbm, acc, in_sem.at[4]),
        pltpu.make_async_copy(exch_hbm, exch, in_sem.at[5]),
    ]

    partners = [flipped(chip, s) for s in range(chips)]
    barrier = pltpu.get_barrier_semaphore()
    pl.semaphore_signal(barrier, inc=1, device_id=(mate, mv), device_id_type=MESH)
    for s in range(1, chips):
        pl.semaphore_signal(barrier, inc=1, device_id=(partners[s] * 2 + core, mv), device_id_type=MESH)
    for s in range(1, nv):
        pl.semaphore_signal(barrier, inc=1, device_id=(me, lax.rem(mv + s, nv)), device_id_type=MESH)

    for load in loads:
        load.start()
    pl.semaphore_wait(barrier, chips + nv - 1)

    def to_mate(s):
        owner = partners[s] * 2 + core
        return pltpu.make_async_remote_copy(
            src_ref=block(owner) if s else int_hbm, dst_ref=block(owner),
            send_sem=core_send.at[s], recv_sem=core_recv.at[s],
            device_id=(mate, mv), device_id_type=MESH,
        )

    def to_chip(s):
        return pltpu.make_async_remote_copy(
            src_ref=int_hbm, dst_ref=block(me),
            send_sem=chip_send.at[s], recv_sem=chip_recv.at[s],
            device_id=(partners[s] * 2 + core, mv), device_id_type=MESH,
        )

    def from_chip(s):
        owner = partners[s] * 2 + core
        return pltpu.make_async_remote_copy(
            src_ref=block(owner), dst_ref=block(owner),
            send_sem=chip_send.at[s], recv_sem=chip_recv.at[s],
            device_id=(partners[s] * 2 + core, mv), device_id_type=MESH,
        )

    def from_mate(s):
        owner = partners[s] * 2 + (1 - core)
        return pltpu.make_async_remote_copy(
            src_ref=block(owner), dst_ref=block(owner),
            send_sem=core_send.at[s], recv_sem=core_recv.at[s],
            device_id=(mate, mv), device_id_type=MESH,
        )

    chip_copies = [None] + [to_chip(s) for s in range(1, chips)]
    mate_copies = [to_mate(s) for s in range(chips)]
    for s in range(1, chips):
        chip_copies[s].start()
    mate_copies[0].start()

    loads[2].wait()
    loads[3].wait()
    for r in range(rows // PTILE):
        tall = pl.ds(r * PTILE, PTILE)
        for k in range(amp.shape[1] // VTILE):
            wide = pl.ds(k * VTILE, VTILE)
            keep = amap[r, k].astype(jnp.float32).astype(jnp.bfloat16)
            amp[tall, wide] = amp[tall, wide] * keep
    loads[4].wait()
    loads[5].wait()

    loads[0].wait()
    loads[1].wait()
    span = 2 * depth
    grain = min(span, VTILE)
    while span % grain or VTILE % grain:
        grain //= 2

    def product(s):
        start = partners[s] * span
        for t in range(span // grain):
            tile = (start + t * grain) // VTILE
            here = pl.ds(pl.multiple_of(start + t * grain, grain), grain)
            for c in range(cols // VTILE):
                wide = pl.ds(c * VTILE, VTILE)
                keep = imap[c, tile].astype(jnp.float32).astype(jnp.bfloat16)
                screened[pl.ds(t * grain, grain), wide] = panel[here, wide] * keep
        return jnp.dot(
            amp[:, pl.ds(pl.multiple_of(start, LANES), span)], screened[...],
            preferred_element_type=jnp.float32,
        )

    for s in range(chips):
        if s + 1 < chips:
            if s == 0:
                from_mate(0).wait_recv()
                acc[...] += product(0)
            from_chip(s + 1).wait_recv()
            mate_copies[s + 1].start()
        if s > 0:
            from_mate(s).wait_recv()
            if s < chips - 1:
                acc[...] += product(s)

    residual = acc[...] + product(chips - 1)
    out_ref[...] = residual
    terms = residual * exch[...].astype(jnp.float32)
    folded = terms[:, :LANES]
    for c in range(1, cols // LANES):
        folded = folded + terms[:, c * LANES:(c + 1) * LANES]
    for q in range(rows // LANES):
        part = folded[q * LANES:(q + 1) * LANES, :].T
        slots[mv, pl.ds(q, 1), :] = jnp.sum(part, axis=0, keepdims=True)

    sends = []
    for s in range(1, nv):
        send = pltpu.make_async_remote_copy(
            src_ref=slots.at[mv], dst_ref=slots.at[mv],
            send_sem=en_send.at[s], recv_sem=en_recv.at[s],
            device_id=(me, lax.rem(mv + s, nv)), device_id_type=MESH,
        )
        send.start()
        sends.append(send)
    for s in range(1, nv):
        origin = lax.rem(mv + nv - s, nv)
        pltpu.make_async_remote_copy(
            src_ref=slots.at[origin], dst_ref=slots.at[origin],
            send_sem=en_send.at[s], recv_sem=en_recv.at[s],
            device_id=(me, origin), device_id_type=MESH,
        ).wait_recv()
    total = slots[0]
    for v in range(1, nv):
        total = total + slots[v]
    energy_ref[...] = total

    for send in sends:
        send.wait_send()
    for s in range(1, chips):
        chip_copies[s].wait_send()
    for s in range(chips):
        mate_copies[s].wait_send()


def deliver(residual, energy, residual_out, energy_out, sem):
    copies = [
        pltpu.make_async_copy(residual, residual_out, sem.at[0]),
        pltpu.make_async_copy(energy, energy_out, sem.at[1]),
    ]
    for copy in copies:
        copy.start()
    for copy in copies:
        copy.wait()


def solution(mesh):
    n, nv = mesh.shape["occ"], mesh.shape["virt"]
    chips = n // 2

    def on_device(amplitudes, amp_map, integrals, int_map, exchange, residual_in):
        rows, k = amplitudes.shape
        depth, cols = integrals.shape
        imap = int_map.T
        held = 2 * rows * k + 2 * k * cols + 2 * rows * cols + 8 * rows * cols
        hbm = pl.BlockSpec(memory_space=pltpu.HBM)
        vmem = pl.BlockSpec(memory_space=pltpu.VMEM)
        residual, energy = pl.pallas_call(
            functools.partial(kernel, n, nv),
            out_shape=(
                pltpu.VMEM((rows, cols), jnp.float32),
                pltpu.VMEM((rows // LANES, LANES), jnp.float32),
            ),
            in_specs=[hbm] * 6,
            out_specs=(vmem, vmem),
            scratch_shapes=[
                pltpu.VMEM((rows, k), jnp.bfloat16),
                pltpu.SMEM(amp_map.shape, jnp.int32),
                pltpu.VMEM((k, cols), jnp.bfloat16),
                pltpu.VMEM((2 * depth, cols), jnp.bfloat16),
                pltpu.SMEM(imap.shape, jnp.int32),
                pltpu.VMEM((rows, cols), jnp.bfloat16),
                pltpu.VMEM((rows, cols), jnp.float32),
                pltpu.VMEM((nv, rows // LANES, LANES), jnp.float32),
                pltpu.SemaphoreType.DMA((6,)),
                pltpu.SemaphoreType.DMA((chips,)),
                pltpu.SemaphoreType.DMA((chips,)),
                pltpu.SemaphoreType.DMA((chips,)),
                pltpu.SemaphoreType.DMA((chips,)),
                pltpu.SemaphoreType.DMA((nv,)),
                pltpu.SemaphoreType.DMA((nv,)),
            ],
            compiler_params=pltpu.CompilerParams(
                collective_id=0, has_side_effects=True, vmem_limit_bytes=held + (8 << 20)
            ),
            cost_estimate=pl.CostEstimate(flops=2 * rows * k * cols, bytes_accessed=held, transcendentals=0),
        )(*(pltpu.with_memory_space_constraint(x, pltpu.HBM) for x in (amplitudes, amp_map, integrals, imap, exchange, residual_in)))
        residual, energy = pl.pallas_call(
            deliver,
            out_shape=(
                jax.ShapeDtypeStruct((rows, cols), jnp.float32),
                jax.ShapeDtypeStruct((rows // LANES, LANES), jnp.float32),
            ),
            in_specs=[vmem, vmem],
            out_specs=(hbm, hbm),
            scratch_shapes=[pltpu.SemaphoreType.DMA((2,))],
        )(residual, energy)
        return residual, energy.reshape(rows)

    in_specs = (
        P("occ", None),
        P("occ", None),
        P("occ", "virt"),
        P(None, "virt"),
        P("occ", "virt"),
        P("occ", "virt"),
    )
    out_specs = (P("occ", "virt"), P("occ"))
    return jax.shard_map(on_device, mesh=mesh, in_specs=in_specs, out_specs=out_specs, check_vma=False)
```

```python
import functools

import jax
import jax.numpy as jnp
from jax import lax
from jax.experimental import pallas as pl
from jax.experimental.pallas import tpu as pltpu
from jax.sharding import PartitionSpec as P

PTILE = 64
VTILE = 128
LANES = 128
MESH = pl.DeviceIdType.MESH


def flipped(index, bits):
    out, place = 0, 1
    top = 0
    while place <= bits:
        digit = lax.rem(index // place, 2)
        flip = (bits // place) % 2
        out = out + (1 - digit if flip else digit) * place
        place *= 2
        top = place
    return out + (index // top) * top if top else index


def kernel(
    n, nv,
    amp_hbm, amap_hbm, int_hbm, imap_hbm, exch_hbm, res_hbm,
    out_ref, energy_ref,
    amp, amap, panel, screened, imap, exch, acc, slots,
    in_sem, core_send, core_recv, chip_send, chip_recv, en_send, en_recv,
):
    me = lax.axis_index("occ")
    mv = lax.axis_index("virt")
    chips = n // 2
    chip, core = me // 2, lax.rem(me, 2)
    mate = chip * 2 + (1 - core)
    depth = int_hbm.shape[0]
    rows, cols = out_ref.shape

    def block(owner):
        return panel.at[pl.ds(pl.multiple_of(owner * depth, depth), depth), :]

    loads = [
        pltpu.make_async_copy(int_hbm, block(me), in_sem.at[0]),
        pltpu.make_async_copy(imap_hbm, imap, in_sem.at[1]),
        pltpu.make_async_copy(amp_hbm, amp, in_sem.at[2]),
        pltpu.make_async_copy(amap_hbm, amap, in_sem.at[3]),
        pltpu.make_async_copy(res_hbm, acc, in_sem.at[4]),
        pltpu.make_async_copy(exch_hbm, exch, in_sem.at[5]),
    ]

    partners = [flipped(chip, s) for s in range(chips)]
    barrier = pltpu.get_barrier_semaphore()
    pl.semaphore_signal(barrier, inc=1, device_id=(mate, mv), device_id_type=MESH)
    for s in range(1, chips):
        pl.semaphore_signal(barrier, inc=1, device_id=(partners[s] * 2 + core, mv), device_id_type=MESH)
    for s in range(1, nv):
        pl.semaphore_signal(barrier, inc=1, device_id=(me, lax.rem(mv + s, nv)), device_id_type=MESH)

    pl.semaphore_wait(barrier, chips + nv - 1)

    def to_mate(s):
        owner = partners[s] * 2 + core
        return pltpu.make_async_remote_copy(
            src_ref=block(owner) if s else int_hbm, dst_ref=block(owner),
            send_sem=core_send.at[s], recv_sem=core_recv.at[s],
            device_id=(mate, mv), device_id_type=MESH,
        )

    def to_chip(s):
        return pltpu.make_async_remote_copy(
            src_ref=int_hbm, dst_ref=block(me),
            send_sem=chip_send.at[s], recv_sem=chip_recv.at[s],
            device_id=(partners[s] * 2 + core, mv), device_id_type=MESH,
        )

    def from_chip(s):
        owner = partners[s] * 2 + core
        return pltpu.make_async_remote_copy(
            src_ref=block(owner), dst_ref=block(owner),
            send_sem=chip_send.at[s], recv_sem=chip_recv.at[s],
            device_id=(partners[s] * 2 + core, mv), device_id_type=MESH,
        )

    def from_mate(s):
        owner = partners[s] * 2 + (1 - core)
        return pltpu.make_async_remote_copy(
            src_ref=block(owner), dst_ref=block(owner),
            send_sem=core_send.at[s], recv_sem=core_recv.at[s],
            device_id=(mate, mv), device_id_type=MESH,
        )

    chip_copies = [None] + [to_chip(s) for s in range(1, chips)]
    mate_copies = [to_mate(s) for s in range(chips)]
    for s in range(1, chips):
        chip_copies[s].start()
    mate_copies[0].start()
    for load in loads:
        load.start()

    loads[2].wait()
    loads[3].wait()
    for r in range(rows // PTILE):
        tall = pl.ds(r * PTILE, PTILE)
        for k in range(amp.shape[1] // VTILE):
            wide = pl.ds(k * VTILE, VTILE)
            keep = amap[r, k].astype(jnp.float32).astype(jnp.bfloat16)
            amp[tall, wide] = amp[tall, wide] * keep
    loads[4].wait()
    loads[5].wait()

    loads[0].wait()
    loads[1].wait()
    span = 2 * depth
    grain = min(span, VTILE)
    while span % grain or VTILE % grain:
        grain //= 2

    def product(s):
        start = partners[s] * span
        for t in range(span // grain):
            tile = (start + t * grain) // VTILE
            here = pl.ds(pl.multiple_of(start + t * grain, grain), grain)
            for c in range(cols // VTILE):
                wide = pl.ds(c * VTILE, VTILE)
                keep = imap[c, tile].astype(jnp.float32).astype(jnp.bfloat16)
                screened[pl.ds(t * grain, grain), wide] = panel[here, wide] * keep
        return jnp.dot(
            amp[:, pl.ds(pl.multiple_of(start, LANES), span)], screened[...],
            preferred_element_type=jnp.float32,
        )

    for s in range(chips):
        if s + 1 < chips:
            if s == 0:
                from_mate(0).wait_recv()
                acc[...] += product(0)
            from_chip(s + 1).wait_recv()
            mate_copies[s + 1].start()
        if s > 0:
            from_mate(s).wait_recv()
            if s < chips - 1:
                acc[...] += product(s)

    residual = acc[...] + product(chips - 1)
    out_ref[...] = residual
    terms = residual * exch[...].astype(jnp.float32)
    folded = terms[:, :LANES]
    for c in range(1, cols // LANES):
        folded = folded + terms[:, c * LANES:(c + 1) * LANES]
    for q in range(rows // LANES):
        part = folded[q * LANES:(q + 1) * LANES, :].T
        slots[mv, pl.ds(q, 1), :] = jnp.sum(part, axis=0, keepdims=True)

    sends = []
    for s in range(1, nv):
        send = pltpu.make_async_remote_copy(
            src_ref=slots.at[mv], dst_ref=slots.at[mv],
            send_sem=en_send.at[s], recv_sem=en_recv.at[s],
            device_id=(me, lax.rem(mv + s, nv)), device_id_type=MESH,
        )
        send.start()
        sends.append(send)
    for s in range(1, nv):
        origin = lax.rem(mv + nv - s, nv)
        pltpu.make_async_remote_copy(
            src_ref=slots.at[origin], dst_ref=slots.at[origin],
            send_sem=en_send.at[s], recv_sem=en_recv.at[s],
            device_id=(me, origin), device_id_type=MESH,
        ).wait_recv()
    total = slots[0]
    for v in range(1, nv):
        total = total + slots[v]
    energy_ref[...] = total

    for send in sends:
        send.wait_send()
    for s in range(1, chips):
        chip_copies[s].wait_send()
    for s in range(chips):
        mate_copies[s].wait_send()


def deliver(residual, energy, residual_out, energy_out, sem):
    copies = [
        pltpu.make_async_copy(residual, residual_out, sem.at[0]),
        pltpu.make_async_copy(energy, energy_out, sem.at[1]),
    ]
    for copy in copies:
        copy.start()
    for copy in copies:
        copy.wait()


def solution(mesh):
    n, nv = mesh.shape["occ"], mesh.shape["virt"]
    chips = n // 2

    def on_device(amplitudes, amp_map, integrals, int_map, exchange, residual_in):
        rows, k = amplitudes.shape
        depth, cols = integrals.shape
        imap = int_map.T
        held = 2 * rows * k + 2 * k * cols + 2 * rows * cols + 8 * rows * cols
        hbm = pl.BlockSpec(memory_space=pltpu.HBM)
        vmem = pl.BlockSpec(memory_space=pltpu.VMEM)
        residual, energy = pl.pallas_call(
            functools.partial(kernel, n, nv),
            out_shape=(
                pltpu.VMEM((rows, cols), jnp.float32),
                pltpu.VMEM((rows // LANES, LANES), jnp.float32),
            ),
            in_specs=[hbm] * 6,
            out_specs=(vmem, vmem),
            scratch_shapes=[
                pltpu.VMEM((rows, k), jnp.bfloat16),
                pltpu.SMEM(amp_map.shape, jnp.int32),
                pltpu.VMEM((k, cols), jnp.bfloat16),
                pltpu.VMEM((2 * depth, cols), jnp.bfloat16),
                pltpu.SMEM(imap.shape, jnp.int32),
                pltpu.VMEM((rows, cols), jnp.bfloat16),
                pltpu.VMEM((rows, cols), jnp.float32),
                pltpu.VMEM((nv, rows // LANES, LANES), jnp.float32),
                pltpu.SemaphoreType.DMA((6,)),
                pltpu.SemaphoreType.DMA((chips,)),
                pltpu.SemaphoreType.DMA((chips,)),
                pltpu.SemaphoreType.DMA((chips,)),
                pltpu.SemaphoreType.DMA((chips,)),
                pltpu.SemaphoreType.DMA((nv,)),
                pltpu.SemaphoreType.DMA((nv,)),
            ],
            compiler_params=pltpu.CompilerParams(
                collective_id=0, has_side_effects=True, vmem_limit_bytes=held + (8 << 20)
            ),
            cost_estimate=pl.CostEstimate(flops=2 * rows * k * cols, bytes_accessed=held, transcendentals=0),
        )(*(pltpu.with_memory_space_constraint(x, pltpu.HBM) for x in (amplitudes, amp_map, integrals, imap, exchange, residual_in)))
        residual, energy = pl.pallas_call(
            deliver,
            out_shape=(
                jax.ShapeDtypeStruct((rows, cols), jnp.float32),
                jax.ShapeDtypeStruct((rows // LANES, LANES), jnp.float32),
            ),
            in_specs=[vmem, vmem],
            out_specs=(hbm, hbm),
            scratch_shapes=[pltpu.SemaphoreType.DMA((2,))],
        )(*(pltpu.with_memory_space_constraint(x, pltpu.VMEM) for x in (residual, energy)))
        return residual, energy.reshape(rows)

    in_specs = (
        P("occ", None),
        P("occ", None),
        P("occ", "virt"),
        P(None, "virt"),
        P("occ", "virt"),
        P("occ", "virt"),
    )
    out_specs = (P("occ", "virt"), P("occ"))
    return jax.shard_map(on_device, mesh=mesh, in_specs=in_specs, out_specs=out_specs, check_vma=False)
```

```python
import functools

import jax
import jax.numpy as jnp
from jax import lax
from jax.experimental import pallas as pl
from jax.experimental.pallas import tpu as pltpu
from jax.sharding import PartitionSpec as P

PTILE = 64
VTILE = 128
LANES = 128
MESH = pl.DeviceIdType.MESH


def flipped(index, bits):
    out, place = 0, 1
    top = 0
    while place <= bits:
        digit = lax.rem(index // place, 2)
        flip = (bits // place) % 2
        out = out + (1 - digit if flip else digit) * place
        place *= 2
        top = place
    return out + (index // top) * top if top else index


def kernel(
    n, nv,
    amp_hbm, amap_hbm, int_hbm, imap_hbm, exch_hbm, res_hbm,
    out_ref, energy_ref,
    amp, amap, panel, screened, imap, exch, acc, slots,
    in_sem, core_send, core_recv, chip_send, chip_recv, en_send, en_recv,
):
    me = lax.axis_index("occ")
    mv = lax.axis_index("virt")
    chips = n // 2
    chip, core = me // 2, lax.rem(me, 2)
    mate = chip * 2 + (1 - core)
    depth = int_hbm.shape[0]
    rows, cols = out_ref.shape

    def block(owner):
        return panel.at[pl.ds(pl.multiple_of(owner * depth, depth), depth), :]

    loads = [
        pltpu.make_async_copy(int_hbm, block(me), in_sem.at[0]),
        pltpu.make_async_copy(imap_hbm, imap, in_sem.at[1]),
        pltpu.make_async_copy(amp_hbm, amp, in_sem.at[2]),
        pltpu.make_async_copy(amap_hbm, amap, in_sem.at[3]),
        pltpu.make_async_copy(res_hbm, acc, in_sem.at[4]),
        pltpu.make_async_copy(exch_hbm, exch, in_sem.at[5]),
    ]

    partners = [flipped(chip, s) for s in range(chips)]
    barrier = pltpu.get_barrier_semaphore()
    pl.semaphore_signal(barrier, inc=1, device_id=(mate, mv), device_id_type=MESH)
    relayed = chips == 4
    greeted = (1, 2) if relayed else tuple(range(1, chips))
    for s in greeted:
        pl.semaphore_signal(barrier, inc=1, device_id=(partners[s] * 2 + core, mv), device_id_type=MESH)
    for s in range(1, nv):
        pl.semaphore_signal(barrier, inc=1, device_id=(me, lax.rem(mv + s, nv)), device_id_type=MESH)

    pl.semaphore_wait(barrier, len(greeted) + nv)

    def push(owner, part, target, send, recv):
        low, size = part
        here = panel.at[pl.ds(pl.multiple_of(owner * depth + low, 16), size), :]
        source = int_hbm.at[pl.ds(low, size), :] if owner is me else here
        return pltpu.make_async_remote_copy(
            src_ref=source, dst_ref=here, send_sem=send, recv_sem=recv,
            device_id=(target, mv), device_id_type=MESH,
        )

    full, top, bottom = (0, depth), (0, depth // 2), (depth // 2, depth - depth // 2)
    theirs = [p * 2 + core for p in partners]
    theirs[0] = me
    others = [p * 2 + (1 - core) for p in partners]

    def to_mate(s, part=full, k=0):
        return push(theirs[s], part, mate, core_send.at[s, k], core_recv.at[s, k])

    def from_mate(s, part=full, k=0):
        return push(others[s], part, mate, core_send.at[s, k], core_recv.at[s, k])

    def to_chip(s, part=full, k=0):
        return push(me, part, theirs[s], chip_send.at[s, k], chip_recv.at[s, k])

    def from_chip(s, part=full, k=0):
        return push(theirs[s], part, theirs[s], chip_send.at[s, k], chip_recv.at[s, k])

    sent = []

    def go(copy):
        copy.start()
        sent.append(copy)

    if relayed:
        go(to_chip(1, top, 0))
        go(to_chip(2, bottom, 1))
        go(to_chip(1, bottom, 1))
        go(to_chip(2, top, 0))
    else:
        for s in range(1, chips):
            go(to_chip(s))
    go(to_mate(0))
    for load in loads:
        load.start()

    if relayed:
        from_chip(1, top, 0).wait_recv()
        go(push(theirs[1], top, theirs[2], chip_send.at[3, 0], chip_recv.at[3, 0]))
        from_chip(2, bottom, 1).wait_recv()
        go(push(theirs[2], bottom, theirs[1], chip_send.at[3, 1], chip_recv.at[3, 1]))
        from_chip(1, bottom, 1).wait_recv()
        go(to_mate(1))
        from_chip(2, top, 0).wait_recv()
        go(to_mate(2))

    loads[2].wait()
    loads[3].wait()
    for r in range(rows // PTILE):
        tall = pl.ds(r * PTILE, PTILE)
        for k in range(amp.shape[1] // VTILE):
            wide = pl.ds(k * VTILE, VTILE)
            keep = amap[r, k].astype(jnp.float32).astype(jnp.bfloat16)
            amp[tall, wide] = amp[tall, wide] * keep
    loads[4].wait()
    loads[5].wait()

    loads[0].wait()
    loads[1].wait()
    span = 2 * depth
    grain = min(span, VTILE)
    while span % grain or VTILE % grain:
        grain //= 2

    def product(s):
        start = partners[s] * span
        for t in range(span // grain):
            tile = (start + t * grain) // VTILE
            here = pl.ds(pl.multiple_of(start + t * grain, grain), grain)
            for c in range(cols // VTILE):
                wide = pl.ds(c * VTILE, VTILE)
                keep = imap[c, tile].astype(jnp.float32).astype(jnp.bfloat16)
                screened[pl.ds(t * grain, grain), wide] = panel[here, wide] * keep
        return jnp.dot(
            amp[:, pl.ds(pl.multiple_of(start, LANES), span)], screened[...],
            preferred_element_type=jnp.float32,
        )

    if relayed:
        from_mate(0).wait_recv()
        acc[...] += product(0)
        push(theirs[3], top, theirs[2], chip_send.at[3, 0], chip_recv.at[3, 0]).wait_recv()
        go(to_mate(3, top, 0))
        push(theirs[3], bottom, theirs[1], chip_send.at[3, 1], chip_recv.at[3, 1]).wait_recv()
        go(to_mate(3, bottom, 1))
        for s in (1, 2):
            from_mate(s).wait_recv()
            acc[...] += product(s)
        from_mate(3, top, 0).wait_recv()
        from_mate(3, bottom, 1).wait_recv()
    else:
        from_mate(0).wait_recv()
        if chips > 1:
            acc[...] += product(0)
        for s in range(1, chips):
            from_chip(s).wait_recv()
            go(to_mate(s))
            if s > 1:
                from_mate(s - 1).wait_recv()
                acc[...] += product(s - 1)
        if chips > 1:
            from_mate(chips - 1).wait_recv()

    residual = acc[...] + product(chips - 1)
    out_ref[...] = residual
    terms = residual * exch[...].astype(jnp.float32)
    folded = terms[:, :LANES]
    for c in range(1, cols // LANES):
        folded = folded + terms[:, c * LANES:(c + 1) * LANES]
    for q in range(rows // LANES):
        part = folded[q * LANES:(q + 1) * LANES, :].T
        slots[mv, pl.ds(q, 1), :] = jnp.sum(part, axis=0, keepdims=True)

    for s in range(1, nv):
        go(pltpu.make_async_remote_copy(
            src_ref=slots.at[mv], dst_ref=slots.at[mv],
            send_sem=en_send.at[s], recv_sem=en_recv.at[s],
            device_id=(me, lax.rem(mv + s, nv)), device_id_type=MESH,
        ))
    for s in range(1, nv):
        origin = lax.rem(mv + nv - s, nv)
        pltpu.make_async_remote_copy(
            src_ref=slots.at[origin], dst_ref=slots.at[origin],
            send_sem=en_send.at[s], recv_sem=en_recv.at[s],
            device_id=(me, origin), device_id_type=MESH,
        ).wait_recv()
    total = slots[0]
    for v in range(1, nv):
        total = total + slots[v]
    energy_ref[...] = total

    for copy in sent:
        copy.wait_send()


def deliver(residual, energy, residual_out, energy_out, sem):
    copies = [
        pltpu.make_async_copy(residual, residual_out, sem.at[0]),
        pltpu.make_async_copy(energy, energy_out, sem.at[1]),
    ]
    for copy in copies:
        copy.start()
    for copy in copies:
        copy.wait()


def solution(mesh):
    n, nv = mesh.shape["occ"], mesh.shape["virt"]
    chips = n // 2

    def on_device(amplitudes, amp_map, integrals, int_map, exchange, residual_in):
        rows, k = amplitudes.shape
        depth, cols = integrals.shape
        imap = int_map.T
        held = 2 * rows * k + 2 * k * cols + 2 * rows * cols + 8 * rows * cols
        hbm = pl.BlockSpec(memory_space=pltpu.HBM)
        vmem = pl.BlockSpec(memory_space=pltpu.VMEM)
        residual, energy = pl.pallas_call(
            functools.partial(kernel, n, nv),
            out_shape=(
                pltpu.VMEM((rows, cols), jnp.float32),
                pltpu.VMEM((rows // LANES, LANES), jnp.float32),
            ),
            in_specs=[hbm] * 6,
            out_specs=(vmem, vmem),
            scratch_shapes=[
                pltpu.VMEM((rows, k), jnp.bfloat16),
                pltpu.SMEM(amp_map.shape, jnp.int32),
                pltpu.VMEM((k, cols), jnp.bfloat16),
                pltpu.VMEM((2 * depth, cols), jnp.bfloat16),
                pltpu.SMEM(imap.shape, jnp.int32),
                pltpu.VMEM((rows, cols), jnp.bfloat16),
                pltpu.VMEM((rows, cols), jnp.float32),
                pltpu.VMEM((nv, rows // LANES, LANES), jnp.float32),
                pltpu.SemaphoreType.DMA((6,)),
                pltpu.SemaphoreType.DMA((chips, 2)),
                pltpu.SemaphoreType.DMA((chips, 2)),
                pltpu.SemaphoreType.DMA((chips, 2)),
                pltpu.SemaphoreType.DMA((chips, 2)),
                pltpu.SemaphoreType.DMA((nv,)),
                pltpu.SemaphoreType.DMA((nv,)),
            ],
            compiler_params=pltpu.CompilerParams(
                collective_id=0, has_side_effects=True, vmem_limit_bytes=held + (8 << 20)
            ),
            cost_estimate=pl.CostEstimate(flops=2 * rows * k * cols, bytes_accessed=held, transcendentals=0),
        )(*(pltpu.with_memory_space_constraint(x, pltpu.HBM) for x in (amplitudes, amp_map, integrals, imap, exchange, residual_in)))
        residual, energy = pl.pallas_call(
            deliver,
            out_shape=(
                jax.ShapeDtypeStruct((rows, cols), jnp.float32),
                jax.ShapeDtypeStruct((rows // LANES, LANES), jnp.float32),
            ),
            in_specs=[vmem, vmem],
            out_specs=(hbm, hbm),
            scratch_shapes=[pltpu.SemaphoreType.DMA((2,))],
        )(*(pltpu.with_memory_space_constraint(x, pltpu.VMEM) for x in (residual, energy)))
        return residual, energy.reshape(rows)

    in_specs = (
        P("occ", None),
        P("occ", None),
        P("occ", "virt"),
        P(None, "virt"),
        P("occ", "virt"),
        P("occ", "virt"),
    )
    out_specs = (P("occ", "virt"), P("occ"))
    return jax.shard_map(on_device, mesh=mesh, in_specs=in_specs, out_specs=out_specs, check_vma=False)
```

```python
import functools

import jax
import jax.numpy as jnp
from jax import lax
from jax.experimental import pallas as pl
from jax.experimental.pallas import tpu as pltpu
from jax.sharding import PartitionSpec as P

PTILE = 64
VTILE = 128
LANES = 128
MESH = pl.DeviceIdType.MESH


def flipped(index, bits):
    out, place = 0, 1
    top = 0
    while place <= bits:
        digit = lax.rem(index // place, 2)
        flip = (bits // place) % 2
        out = out + (1 - digit if flip else digit) * place
        place *= 2
        top = place
    return out + (index // top) * top if top else index


def kernel(
    n, nv,
    amp_hbm, amap_hbm, int_hbm, imap_hbm, exch_hbm, res_hbm,
    out_ref, energy_ref,
    amp, amap, panel, screened, imap, exch, acc, slots,
    in_sem, core_send, core_recv, chip_send, chip_recv, en_send, en_recv,
):
    me = lax.axis_index("occ")
    mv = lax.axis_index("virt")
    chips = n // 2
    chip, core = me // 2, lax.rem(me, 2)
    mate = chip * 2 + (1 - core)
    depth = int_hbm.shape[0]
    rows, cols = out_ref.shape

    def block(owner):
        return panel.at[pl.ds(pl.multiple_of(owner * depth, depth), depth), :]

    loads = [
        pltpu.make_async_copy(int_hbm, block(me), in_sem.at[0]),
        pltpu.make_async_copy(imap_hbm, imap, in_sem.at[1]),
        pltpu.make_async_copy(amp_hbm, amp, in_sem.at[2]),
        pltpu.make_async_copy(amap_hbm, amap, in_sem.at[3]),
        pltpu.make_async_copy(res_hbm, acc, in_sem.at[4]),
        pltpu.make_async_copy(exch_hbm, exch, in_sem.at[5]),
    ]

    partners = [flipped(chip, s) for s in range(chips)]
    barrier = pltpu.get_barrier_semaphore()
    pl.semaphore_signal(barrier, inc=1, device_id=(mate, mv), device_id_type=MESH)
    for s in range(1, chips):
        pl.semaphore_signal(barrier, inc=1, device_id=(partners[s] * 2 + core, mv), device_id_type=MESH)
    for s in range(1, nv):
        pl.semaphore_signal(barrier, inc=1, device_id=(me, lax.rem(mv + s, nv)), device_id_type=MESH)

    pl.semaphore_wait(barrier, chips + nv - 1)

    def push(owner, target, send, recv):
        return pltpu.make_async_remote_copy(
            src_ref=int_hbm if owner is me else block(owner), dst_ref=block(owner),
            send_sem=send, recv_sem=recv, device_id=(target, mv), device_id_type=MESH,
        )

    theirs = [p * 2 + core for p in partners]
    theirs[0] = me
    others = [p * 2 + (1 - core) for p in partners]

    def to_mate(s):
        return push(theirs[s], mate, core_send.at[s], core_recv.at[s])

    def from_mate(s):
        return push(others[s], mate, core_send.at[s], core_recv.at[s])

    def to_chip(s):
        return push(me, theirs[s], chip_send.at[s], chip_recv.at[s])

    def from_chip(s):
        return push(theirs[s], theirs[s], chip_send.at[s], chip_recv.at[s])

    sent = []

    def go(copy):
        copy.start()
        sent.append(copy)

    for s in reversed(range(1, chips)):
        go(to_chip(s))
    go(to_mate(0))
    for load in loads:
        load.start()

    loads[2].wait()
    loads[3].wait()
    for r in range(rows // PTILE):
        tall = pl.ds(r * PTILE, PTILE)
        for k in range(amp.shape[1] // VTILE):
            wide = pl.ds(k * VTILE, VTILE)
            keep = amap[r, k].astype(jnp.float32).astype(jnp.bfloat16)
            amp[tall, wide] = amp[tall, wide] * keep
    loads[4].wait()
    loads[5].wait()

    loads[0].wait()
    loads[1].wait()
    span = 2 * depth
    grain = min(span, VTILE)
    while span % grain or VTILE % grain:
        grain //= 2

    def product(s):
        start = partners[s] * span
        for t in range(span // grain):
            tile = (start + t * grain) // VTILE
            here = pl.ds(pl.multiple_of(start + t * grain, grain), grain)
            for c in range(cols // VTILE):
                wide = pl.ds(c * VTILE, VTILE)
                keep = imap[c, tile].astype(jnp.float32).astype(jnp.bfloat16)
                screened[pl.ds(t * grain, grain), wide] = panel[here, wide] * keep
        return jnp.dot(
            amp[:, pl.ds(pl.multiple_of(start, LANES), span)], screened[...],
            preferred_element_type=jnp.float32,
        )

    for s in range(1, chips):
        from_chip(s).wait_recv()
        go(to_mate(s))
    for s in range(chips):
        from_mate(s).wait_recv()
        if s < chips - 1:
            acc[...] += product(s)

    residual = acc[...] + product(chips - 1)
    out_ref[...] = residual
    terms = residual * exch[...].astype(jnp.float32)
    folded = terms[:, :LANES]
    for c in range(1, cols // LANES):
        folded = folded + terms[:, c * LANES:(c + 1) * LANES]
    for q in range(rows // LANES):
        part = folded[q * LANES:(q + 1) * LANES, :].T
        slots[mv, pl.ds(q, 1), :] = jnp.sum(part, axis=0, keepdims=True)

    for s in range(1, nv):
        go(pltpu.make_async_remote_copy(
            src_ref=slots.at[mv], dst_ref=slots.at[mv],
            send_sem=en_send.at[s], recv_sem=en_recv.at[s],
            device_id=(me, lax.rem(mv + s, nv)), device_id_type=MESH,
        ))
    for s in range(1, nv):
        origin = lax.rem(mv + nv - s, nv)
        pltpu.make_async_remote_copy(
            src_ref=slots.at[origin], dst_ref=slots.at[origin],
            send_sem=en_send.at[s], recv_sem=en_recv.at[s],
            device_id=(me, origin), device_id_type=MESH,
        ).wait_recv()
    total = slots[0]
    for v in range(1, nv):
        total = total + slots[v]
    energy_ref[...] = total

    for copy in sent:
        copy.wait_send()


def deliver(residual, energy, residual_out, energy_out, sem):
    copies = [
        pltpu.make_async_copy(residual, residual_out, sem.at[0]),
        pltpu.make_async_copy(energy, energy_out, sem.at[1]),
    ]
    for copy in copies:
        copy.start()
    for copy in copies:
        copy.wait()


def solution(mesh):
    n, nv = mesh.shape["occ"], mesh.shape["virt"]
    chips = n // 2

    def on_device(amplitudes, amp_map, integrals, int_map, exchange, residual_in):
        rows, k = amplitudes.shape
        depth, cols = integrals.shape
        imap = int_map.T
        held = 2 * rows * k + 2 * k * cols + 2 * rows * cols + 8 * rows * cols
        hbm = pl.BlockSpec(memory_space=pltpu.HBM)
        vmem = pl.BlockSpec(memory_space=pltpu.VMEM)
        residual, energy = pl.pallas_call(
            functools.partial(kernel, n, nv),
            out_shape=(
                pltpu.VMEM((rows, cols), jnp.float32),
                pltpu.VMEM((rows // LANES, LANES), jnp.float32),
            ),
            in_specs=[hbm] * 6,
            out_specs=(vmem, vmem),
            scratch_shapes=[
                pltpu.VMEM((rows, k), jnp.bfloat16),
                pltpu.SMEM(amp_map.shape, jnp.int32),
                pltpu.VMEM((k, cols), jnp.bfloat16),
                pltpu.VMEM((2 * depth, cols), jnp.bfloat16),
                pltpu.SMEM(imap.shape, jnp.int32),
                pltpu.VMEM((rows, cols), jnp.bfloat16),
                pltpu.VMEM((rows, cols), jnp.float32),
                pltpu.VMEM((nv, rows // LANES, LANES), jnp.float32),
                pltpu.SemaphoreType.DMA((6,)),
                pltpu.SemaphoreType.DMA((chips,)),
                pltpu.SemaphoreType.DMA((chips,)),
                pltpu.SemaphoreType.DMA((chips,)),
                pltpu.SemaphoreType.DMA((chips,)),
                pltpu.SemaphoreType.DMA((nv,)),
                pltpu.SemaphoreType.DMA((nv,)),
            ],
            compiler_params=pltpu.CompilerParams(
                collective_id=0, has_side_effects=True, vmem_limit_bytes=held + (8 << 20)
            ),
            cost_estimate=pl.CostEstimate(flops=2 * rows * k * cols, bytes_accessed=held, transcendentals=0),
        )(*(pltpu.with_memory_space_constraint(x, pltpu.HBM) for x in (amplitudes, amp_map, integrals, imap, exchange, residual_in)))
        residual, energy = pl.pallas_call(
            deliver,
            out_shape=(
                jax.ShapeDtypeStruct((rows, cols), jnp.float32),
                jax.ShapeDtypeStruct((rows // LANES, LANES), jnp.float32),
            ),
            in_specs=[vmem, vmem],
            out_specs=(hbm, hbm),
            scratch_shapes=[pltpu.SemaphoreType.DMA((2,))],
        )(*(pltpu.with_memory_space_constraint(x, pltpu.VMEM) for x in (residual, energy)))
        return residual, energy.reshape(rows)

    in_specs = (
        P("occ", None),
        P("occ", None),
        P("occ", "virt"),
        P(None, "virt"),
        P("occ", "virt"),
        P("occ", "virt"),
    )
    out_specs = (P("occ", "virt"), P("occ"))
    return jax.shard_map(on_device, mesh=mesh, in_specs=in_specs, out_specs=out_specs, check_vma=False)
```

```python
import functools

import jax
import jax.numpy as jnp
from jax import lax
from jax.experimental import pallas as pl
from jax.experimental.pallas import tpu as pltpu
from jax.sharding import PartitionSpec as P

PTILE = 64
VTILE = 128
LANES = 128
PARTS = 4
MESH = pl.DeviceIdType.MESH


def flipped(index, bits):
    out, place = 0, 1
    top = 0
    while place <= bits:
        digit = lax.rem(index // place, 2)
        flip = (bits // place) % 2
        out = out + (1 - digit if flip else digit) * place
        place *= 2
        top = place
    return out + (index // top) * top if top else index


def kernel(
    n, nv,
    amp_hbm, amap_hbm, int_hbm, imap_hbm, exch_hbm, res_hbm,
    out_ref, energy_ref,
    amp, amap, panel, screened, imap, exch, acc, slots,
    in_sem, core_send, core_recv, chip_send, chip_recv, en_send, en_recv,
):
    me = lax.axis_index("occ")
    mv = lax.axis_index("virt")
    chips = n // 2
    chip, core = me // 2, lax.rem(me, 2)
    mate = chip * 2 + (1 - core)
    depth = int_hbm.shape[0]
    rows, cols = out_ref.shape

    def block(owner):
        return panel.at[pl.ds(pl.multiple_of(owner * depth, depth), depth), :]

    loads = [
        pltpu.make_async_copy(int_hbm, block(me), in_sem.at[0]),
        pltpu.make_async_copy(imap_hbm, imap, in_sem.at[1]),
        pltpu.make_async_copy(amp_hbm, amp, in_sem.at[2]),
        pltpu.make_async_copy(amap_hbm, amap, in_sem.at[3]),
        pltpu.make_async_copy(res_hbm, acc, in_sem.at[4]),
        pltpu.make_async_copy(exch_hbm, exch, in_sem.at[5]),
    ]

    partners = [flipped(chip, s) for s in range(chips)]
    barrier = pltpu.get_barrier_semaphore()
    for s in reversed(range(1, chips)):
        pl.semaphore_signal(barrier, inc=1, device_id=(partners[s] * 2 + core, mv), device_id_type=MESH)
    pl.semaphore_signal(barrier, inc=1, device_id=(mate, mv), device_id_type=MESH)
    for s in range(1, nv):
        pl.semaphore_signal(barrier, inc=1, device_id=(me, lax.rem(mv + s, nv)), device_id_type=MESH)
    for load in loads:
        load.start()
    loads[0].wait()
    pl.semaphore_wait(barrier, chips + nv - 1)

    def push(owner, target, send, recv):
        return pltpu.make_async_remote_copy(
            src_ref=block(owner), dst_ref=block(owner),
            send_sem=send, recv_sem=recv, device_id=(target, mv), device_id_type=MESH,
        )

    theirs = [p * 2 + core for p in partners]
    theirs[0] = me
    others = [p * 2 + (1 - core) for p in partners]

    def to_mate(s):
        return push(theirs[s], mate, core_send.at[s], core_recv.at[s])

    def from_mate(s):
        return push(others[s], mate, core_send.at[s], core_recv.at[s])

    def to_chip(s):
        return push(me, theirs[s], chip_send.at[s], chip_recv.at[s])

    def from_chip(s):
        return push(theirs[s], theirs[s], chip_send.at[s], chip_recv.at[s])

    sent = []

    def go(copy):
        copy.start()
        sent.append(copy)

    for s in reversed(range(1, chips)):
        go(to_chip(s))
    go(to_mate(0))

    loads[2].wait()
    loads[3].wait()
    for r in range(rows // PTILE):
        tall = pl.ds(r * PTILE, PTILE)
        for k in range(amp.shape[1] // VTILE):
            wide = pl.ds(k * VTILE, VTILE)
            keep = amap[r, k].astype(jnp.float32).astype(jnp.bfloat16)
            amp[tall, wide] = amp[tall, wide] * keep
    loads[4].wait()
    loads[5].wait()
    loads[1].wait()
    span = 2 * depth
    grain = min(span, VTILE)
    while span % grain or VTILE % grain:
        grain //= 2

    def product(s):
        start = partners[s] * span
        for t in range(span // grain):
            tile = (start + t * grain) // VTILE
            here = pl.ds(pl.multiple_of(start + t * grain, grain), grain)
            for c in range(cols // VTILE):
                wide = pl.ds(c * VTILE, VTILE)
                keep = imap[c, tile].astype(jnp.float32).astype(jnp.bfloat16)
                screened[pl.ds(t * grain, grain), wide] = panel[here, wide] * keep
        return jnp.dot(
            amp[:, pl.ds(pl.multiple_of(start, LANES), span)], screened[...],
            preferred_element_type=jnp.float32,
        )

    for s in range(1, chips):
        from_chip(s).wait_recv()
        go(to_mate(s))
    for s in range(chips):
        from_mate(s).wait_recv()
        if s < chips - 1:
            acc[...] += product(s)

    residual = acc[...] + product(chips - 1)
    out_ref[...] = residual
    terms = residual * exch[...].astype(jnp.float32)
    folded = terms[:, :LANES]
    for c in range(1, cols // LANES):
        folded = folded + terms[:, c * LANES:(c + 1) * LANES]
    for q in range(rows // LANES):
        part = folded[q * LANES:(q + 1) * LANES, :].T
        slots[mv, pl.ds(q, 1), :] = jnp.sum(part, axis=0, keepdims=True)

    for s in range(1, nv):
        go(pltpu.make_async_remote_copy(
            src_ref=slots.at[mv], dst_ref=slots.at[mv],
            send_sem=en_send.at[s], recv_sem=en_recv.at[s],
            device_id=(me, lax.rem(mv + s, nv)), device_id_type=MESH,
        ))
    for s in range(1, nv):
        origin = lax.rem(mv + nv - s, nv)
        pltpu.make_async_remote_copy(
            src_ref=slots.at[origin], dst_ref=slots.at[origin],
            send_sem=en_send.at[s], recv_sem=en_recv.at[s],
            device_id=(me, origin), device_id_type=MESH,
        ).wait_recv()
    total = slots[0]
    for v in range(1, nv):
        total = total + slots[v]
    energy_ref[...] = total

    for copy in sent:
        copy.wait_send()


def deliver(residual, energy, residual_out, energy_out, sem):
    part = residual.shape[0] // PARTS
    copies = [pltpu.make_async_copy(energy, energy_out, sem.at[PARTS])]
    for p in range(PARTS):
        here = pl.ds(p * part, part)
        copies.append(pltpu.make_async_copy(residual.at[here, :], residual_out.at[here, :], sem.at[p]))
    for copy in copies:
        copy.start()
    for copy in copies:
        copy.wait()


def solution(mesh):
    n, nv = mesh.shape["occ"], mesh.shape["virt"]
    chips = n // 2

    def on_device(amplitudes, amp_map, integrals, int_map, exchange, residual_in):
        rows, k = amplitudes.shape
        depth, cols = integrals.shape
        imap = int_map.T
        held = 2 * rows * k + 2 * k * cols + 2 * rows * cols + 8 * rows * cols
        hbm = pl.BlockSpec(memory_space=pltpu.HBM)
        vmem = pl.BlockSpec(memory_space=pltpu.VMEM)
        residual, energy = pl.pallas_call(
            functools.partial(kernel, n, nv),
            out_shape=(
                pltpu.VMEM((rows, cols), jnp.float32),
                pltpu.VMEM((rows // LANES, LANES), jnp.float32),
            ),
            in_specs=[hbm] * 6,
            out_specs=(vmem, vmem),
            scratch_shapes=[
                pltpu.VMEM((rows, k), jnp.bfloat16),
                pltpu.SMEM(amp_map.shape, jnp.int32),
                pltpu.VMEM((k, cols), jnp.bfloat16),
                pltpu.VMEM((2 * depth, cols), jnp.bfloat16),
                pltpu.SMEM(imap.shape, jnp.int32),
                pltpu.VMEM((rows, cols), jnp.bfloat16),
                pltpu.VMEM((rows, cols), jnp.float32),
                pltpu.VMEM((nv, rows // LANES, LANES), jnp.float32),
                pltpu.SemaphoreType.DMA((6,)),
                pltpu.SemaphoreType.DMA((chips,)),
                pltpu.SemaphoreType.DMA((chips,)),
                pltpu.SemaphoreType.DMA((chips,)),
                pltpu.SemaphoreType.DMA((chips,)),
                pltpu.SemaphoreType.DMA((nv,)),
                pltpu.SemaphoreType.DMA((nv,)),
            ],
            compiler_params=pltpu.CompilerParams(
                collective_id=0, has_side_effects=True, vmem_limit_bytes=held + (8 << 20)
            ),
            cost_estimate=pl.CostEstimate(flops=2 * rows * k * cols, bytes_accessed=held, transcendentals=0),
        )(*(pltpu.with_memory_space_constraint(x, pltpu.HBM) for x in (amplitudes, amp_map, integrals, imap, exchange, residual_in)))
        residual, energy = pl.pallas_call(
            deliver,
            out_shape=(
                jax.ShapeDtypeStruct((rows, cols), jnp.float32),
                jax.ShapeDtypeStruct((rows // LANES, LANES), jnp.float32),
            ),
            in_specs=[vmem, vmem],
            out_specs=(hbm, hbm),
            scratch_shapes=[pltpu.SemaphoreType.DMA((PARTS + 1,))],
        )(*(pltpu.with_memory_space_constraint(x, pltpu.VMEM) for x in (residual, energy)))
        return residual, energy.reshape(rows)

    in_specs = (
        P("occ", None),
        P("occ", None),
        P("occ", "virt"),
        P(None, "virt"),
        P("occ", "virt"),
        P("occ", "virt"),
    )
    out_specs = (P("occ", "virt"), P("occ"))
    return jax.shard_map(on_device, mesh=mesh, in_specs=in_specs, out_specs=out_specs, check_vma=False)
```

```python
import functools

import jax
import jax.numpy as jnp
from jax import lax
from jax.experimental import pallas as pl
from jax.experimental.pallas import tpu as pltpu
from jax.sharding import PartitionSpec as P

PTILE = 64
VTILE = 128
LANES = 128
PARTS = 4
MESH = pl.DeviceIdType.MESH


def flipped(index, bits):
    out, place = 0, 1
    top = 0
    while place <= bits:
        digit = lax.rem(index // place, 2)
        flip = (bits // place) % 2
        out = out + (1 - digit if flip else digit) * place
        place *= 2
        top = place
    return out + (index // top) * top if top else index


def kernel(
    n, nv,
    amp_hbm, amap_hbm, int_hbm, imap_hbm, exch_hbm, res_hbm,
    out_ref, energy_ref,
    amp, amap, panel, screened, imap, exch, acc, slots,
    in_sem, part_send, part_recv, en_send, en_recv,
):
    me = lax.axis_index("occ")
    mv = lax.axis_index("virt")
    chips = n // 2
    chip, core = me // 2, lax.rem(me, 2)
    depth = int_hbm.shape[0]
    rows, cols = out_ref.shape

    def block(owner):
        return panel.at[pl.ds(pl.multiple_of(owner * depth, depth), depth), :]

    loads = [
        pltpu.make_async_copy(int_hbm, block(me), in_sem.at[0]),
        pltpu.make_async_copy(imap_hbm, imap, in_sem.at[1]),
        pltpu.make_async_copy(amp_hbm, amp, in_sem.at[2]),
        pltpu.make_async_copy(amap_hbm, amap, in_sem.at[3]),
        pltpu.make_async_copy(res_hbm, acc, in_sem.at[4]),
        pltpu.make_async_copy(exch_hbm, exch, in_sem.at[5]),
    ]

    partners = [flipped(chip, s) for s in range(chips)]
    peers = [(partners[s] * 2 + c, 2 * s + f) for s in reversed(range(chips)) for f, c in enumerate((core, 1 - core)) if s or f]
    barrier = pltpu.get_barrier_semaphore()
    for owner, _ in peers:
        pl.semaphore_signal(barrier, inc=1, device_id=(owner, mv), device_id_type=MESH)
    for s in range(1, nv):
        pl.semaphore_signal(barrier, inc=1, device_id=(me, lax.rem(mv + s, nv)), device_id_type=MESH)
    for load in loads:
        load.start()
    loads[0].wait()
    pl.semaphore_wait(barrier, n + nv - 2)

    def push(owner, target, slot):
        return pltpu.make_async_remote_copy(
            src_ref=block(owner), dst_ref=block(owner),
            send_sem=part_send.at[slot], recv_sem=part_recv.at[slot],
            device_id=(target, mv), device_id_type=MESH,
        )

    sent = []

    def go(copy):
        copy.start()
        sent.append(copy)

    for target, slot in peers:
        go(push(me, target, slot))

    loads[2].wait()
    loads[3].wait()
    for r in range(rows // PTILE):
        tall = pl.ds(r * PTILE, PTILE)
        for k in range(amp.shape[1] // VTILE):
            wide = pl.ds(k * VTILE, VTILE)
            keep = amap[r, k].astype(jnp.float32).astype(jnp.bfloat16)
            amp[tall, wide] = amp[tall, wide] * keep
    loads[4].wait()
    loads[5].wait()
    loads[1].wait()
    span = 2 * depth
    grain = min(span, VTILE)
    while span % grain or VTILE % grain:
        grain //= 2

    def product(s):
        start = partners[s] * span
        for t in range(span // grain):
            tile = (start + t * grain) // VTILE
            here = pl.ds(pl.multiple_of(start + t * grain, grain), grain)
            for c in range(cols // VTILE):
                wide = pl.ds(c * VTILE, VTILE)
                keep = imap[c, tile].astype(jnp.float32).astype(jnp.bfloat16)
                screened[pl.ds(t * grain, grain), wide] = panel[here, wide] * keep
        return jnp.dot(
            amp[:, pl.ds(pl.multiple_of(start, LANES), span)], screened[...],
            preferred_element_type=jnp.float32,
        )

    for s in range(chips):
        for owner, slot in peers:
            if slot // 2 == s:
                push(owner, owner, slot).wait_recv()
        if s < chips - 1:
            acc[...] += product(s)

    residual = acc[...] + product(chips - 1)
    out_ref[...] = residual
    terms = residual * exch[...].astype(jnp.float32)
    folded = terms[:, :LANES]
    for c in range(1, cols // LANES):
        folded = folded + terms[:, c * LANES:(c + 1) * LANES]
    for q in range(rows // LANES):
        part = folded[q * LANES:(q + 1) * LANES, :].T
        slots[mv, pl.ds(q, 1), :] = jnp.sum(part, axis=0, keepdims=True)

    for s in range(1, nv):
        go(pltpu.make_async_remote_copy(
            src_ref=slots.at[mv], dst_ref=slots.at[mv],
            send_sem=en_send.at[s], recv_sem=en_recv.at[s],
            device_id=(me, lax.rem(mv + s, nv)), device_id_type=MESH,
        ))
    for s in range(1, nv):
        origin = lax.rem(mv + nv - s, nv)
        pltpu.make_async_remote_copy(
            src_ref=slots.at[origin], dst_ref=slots.at[origin],
            send_sem=en_send.at[s], recv_sem=en_recv.at[s],
            device_id=(me, origin), device_id_type=MESH,
        ).wait_recv()
    total = slots[0]
    for v in range(1, nv):
        total = total + slots[v]
    energy_ref[...] = total

    for copy in sent:
        copy.wait_send()


def deliver(residual, energy, residual_out, energy_out, sem):
    part = residual.shape[0] // PARTS
    copies = [pltpu.make_async_copy(energy, energy_out, sem.at[PARTS])]
    for p in range(PARTS):
        here = pl.ds(p * part, part)
        copies.append(pltpu.make_async_copy(residual.at[here, :], residual_out.at[here, :], sem.at[p]))
    for copy in copies:
        copy.start()
    for copy in copies:
        copy.wait()


def solution(mesh):
    n, nv = mesh.shape["occ"], mesh.shape["virt"]

    def on_device(amplitudes, amp_map, integrals, int_map, exchange, residual_in):
        rows, k = amplitudes.shape
        depth, cols = integrals.shape
        imap = int_map.T
        held = 2 * rows * k + 2 * k * cols + 2 * rows * cols + 8 * rows * cols
        hbm = pl.BlockSpec(memory_space=pltpu.HBM)
        vmem = pl.BlockSpec(memory_space=pltpu.VMEM)
        residual, energy = pl.pallas_call(
            functools.partial(kernel, n, nv),
            out_shape=(
                pltpu.VMEM((rows, cols), jnp.float32),
                pltpu.VMEM((rows // LANES, LANES), jnp.float32),
            ),
            in_specs=[hbm] * 6,
            out_specs=(vmem, vmem),
            scratch_shapes=[
                pltpu.VMEM((rows, k), jnp.bfloat16),
                pltpu.SMEM(amp_map.shape, jnp.int32),
                pltpu.VMEM((k, cols), jnp.bfloat16),
                pltpu.VMEM((2 * depth, cols), jnp.bfloat16),
                pltpu.SMEM(imap.shape, jnp.int32),
                pltpu.VMEM((rows, cols), jnp.bfloat16),
                pltpu.VMEM((rows, cols), jnp.float32),
                pltpu.VMEM((nv, rows // LANES, LANES), jnp.float32),
                pltpu.SemaphoreType.DMA((6,)),
                pltpu.SemaphoreType.DMA((n,)),
                pltpu.SemaphoreType.DMA((n,)),
                pltpu.SemaphoreType.DMA((nv,)),
                pltpu.SemaphoreType.DMA((nv,)),
            ],
            compiler_params=pltpu.CompilerParams(
                collective_id=0, has_side_effects=True, vmem_limit_bytes=held + (8 << 20)
            ),
            cost_estimate=pl.CostEstimate(flops=2 * rows * k * cols, bytes_accessed=held, transcendentals=0),
        )(*(pltpu.with_memory_space_constraint(x, pltpu.HBM) for x in (amplitudes, amp_map, integrals, imap, exchange, residual_in)))
        residual, energy = pl.pallas_call(
            deliver,
            out_shape=(
                jax.ShapeDtypeStruct((rows, cols), jnp.float32),
                jax.ShapeDtypeStruct((rows // LANES, LANES), jnp.float32),
            ),
            in_specs=[vmem, vmem],
            out_specs=(hbm, hbm),
            scratch_shapes=[pltpu.SemaphoreType.DMA((PARTS + 1,))],
        )(*(pltpu.with_memory_space_constraint(x, pltpu.VMEM) for x in (residual, energy)))
        return residual, energy.reshape(rows)

    in_specs = (
        P("occ", None),
        P("occ", None),
        P("occ", "virt"),
        P(None, "virt"),
        P("occ", "virt"),
        P("occ", "virt"),
    )
    out_specs = (P("occ", "virt"), P("occ"))
    return jax.shard_map(on_device, mesh=mesh, in_specs=in_specs, out_specs=out_specs, check_vma=False)
```

```python
import functools

import jax
import jax.numpy as jnp
from jax import lax
from jax.experimental import pallas as pl
from jax.experimental.pallas import tpu as pltpu
from jax.sharding import PartitionSpec as P

PTILE = 64
VTILE = 128
LANES = 128
MESH = pl.DeviceIdType.MESH


def flipped(index, bits):
    out, place = 0, 1
    top = 0
    while place <= bits:
        digit = lax.rem(index // place, 2)
        flip = (bits // place) % 2
        out = out + (1 - digit if flip else digit) * place
        place *= 2
        top = place
    return out + (index // top) * top if top else index


def kernel(
    n, nv,
    amp_hbm, amap_hbm, int_hbm, imap_hbm, exch_hbm, res_hbm,
    out_ref, energy_ref,
    amp, amap, panel, screened, imap, exch, acc, slots,
    in_sem, core_send, core_recv, chip_send, chip_recv, en_send, en_recv,
):
    me = lax.axis_index("occ")
    mv = lax.axis_index("virt")
    chips = n // 2
    chip, core = me // 2, lax.rem(me, 2)
    mate = chip * 2 + (1 - core)
    depth = int_hbm.shape[0]
    rows, cols = out_ref.shape

    def block(owner):
        return panel.at[pl.ds(pl.multiple_of(owner * depth, depth), depth), :]

    loads = [
        pltpu.make_async_copy(int_hbm, block(me), in_sem.at[0]),
        pltpu.make_async_copy(imap_hbm, imap, in_sem.at[1]),
        pltpu.make_async_copy(amp_hbm, amp, in_sem.at[2]),
        pltpu.make_async_copy(amap_hbm, amap, in_sem.at[3]),
        pltpu.make_async_copy(res_hbm, acc, in_sem.at[4]),
        pltpu.make_async_copy(exch_hbm, exch, in_sem.at[5]),
    ]

    partners = [flipped(chip, s) for s in range(chips)]
    barrier = pltpu.get_barrier_semaphore()
    relayed = chips == 4
    greeted = (1, 2) if relayed else tuple(range(1, chips))
    for s in greeted:
        pl.semaphore_signal(barrier, inc=1, device_id=(partners[s] * 2 + core, mv), device_id_type=MESH)
    pl.semaphore_signal(barrier, inc=1, device_id=(mate, mv), device_id_type=MESH)
    for s in range(1, nv):
        pl.semaphore_signal(barrier, inc=1, device_id=(me, lax.rem(mv + s, nv)), device_id_type=MESH)
    for load in loads:
        load.start()
    loads[0].wait()
    pl.semaphore_wait(barrier, len(greeted) + nv)

    def push(owner, part, target, send, recv):
        low, size = part
        here = panel.at[pl.ds(pl.multiple_of(owner * depth + low, 16), size), :]
        return pltpu.make_async_remote_copy(
            src_ref=here, dst_ref=here, send_sem=send, recv_sem=recv,
            device_id=(target, mv), device_id_type=MESH,
        )

    full, top, bottom = (0, depth), (0, depth // 2), (depth // 2, depth - depth // 2)
    theirs = [p * 2 + core for p in partners]
    theirs[0] = me
    others = [p * 2 + (1 - core) for p in partners]

    def to_mate(s, part=full, k=0):
        return push(theirs[s], part, mate, core_send.at[s, k], core_recv.at[s, k])

    def from_mate(s, part=full, k=0):
        return push(others[s], part, mate, core_send.at[s, k], core_recv.at[s, k])

    def to_chip(s, part=full, k=0):
        return push(me, part, theirs[s], chip_send.at[s, k], chip_recv.at[s, k])

    def from_chip(s, part=full, k=0):
        return push(theirs[s], part, theirs[s], chip_send.at[s, k], chip_recv.at[s, k])

    sent = []

    def go(copy):
        copy.start()
        sent.append(copy)

    if relayed:
        go(to_chip(1, top, 0))
        go(to_chip(2, bottom, 1))
        go(to_chip(1, bottom, 1))
        go(to_chip(2, top, 0))
    else:
        for s in range(1, chips):
            go(to_chip(s))
    go(to_mate(0))

    loads[2].wait()
    loads[3].wait()
    for r in range(rows // PTILE):
        tall = pl.ds(r * PTILE, PTILE)
        for k in range(amp.shape[1] // VTILE):
            wide = pl.ds(k * VTILE, VTILE)
            keep = amap[r, k].astype(jnp.float32).astype(jnp.bfloat16)
            amp[tall, wide] = amp[tall, wide] * keep
    loads[4].wait()
    loads[5].wait()
    loads[1].wait()
    span = 2 * depth
    grain = min(span, VTILE)
    while span % grain or VTILE % grain:
        grain //= 2

    def product(s):
        start = partners[s] * span
        for t in range(span // grain):
            tile = (start + t * grain) // VTILE
            here = pl.ds(pl.multiple_of(start + t * grain, grain), grain)
            for c in range(cols // VTILE):
                wide = pl.ds(c * VTILE, VTILE)
                keep = imap[c, tile].astype(jnp.float32).astype(jnp.bfloat16)
                screened[pl.ds(t * grain, grain), wide] = panel[here, wide] * keep
        return jnp.dot(
            amp[:, pl.ds(pl.multiple_of(start, LANES), span)], screened[...],
            preferred_element_type=jnp.float32,
        )

    if relayed:
        from_chip(1, top, 0).wait_recv()
        go(push(theirs[1], top, theirs[2], chip_send.at[3, 0], chip_recv.at[3, 0]))
        from_chip(2, bottom, 1).wait_recv()
        go(push(theirs[2], bottom, theirs[1], chip_send.at[3, 1], chip_recv.at[3, 1]))
        from_chip(1, bottom, 1).wait_recv()
        go(to_mate(1))
        from_chip(2, top, 0).wait_recv()
        go(to_mate(2))

    if relayed:
        from_mate(0).wait_recv()
        acc[...] += product(0)
        push(theirs[3], top, theirs[2], chip_send.at[3, 0], chip_recv.at[3, 0]).wait_recv()
        go(to_mate(3, top, 0))
        push(theirs[3], bottom, theirs[1], chip_send.at[3, 1], chip_recv.at[3, 1]).wait_recv()
        go(to_mate(3, bottom, 1))
        for s in (1, 2):
            from_mate(s).wait_recv()
            acc[...] += product(s)
        from_mate(3, top, 0).wait_recv()
        from_mate(3, bottom, 1).wait_recv()
    else:
        for s in range(1, chips):
            from_chip(s).wait_recv()
            go(to_mate(s))
        for s in range(chips):
            from_mate(s).wait_recv()
            if s < chips - 1:
                acc[...] += product(s)

    residual = acc[...] + product(chips - 1)
    out_ref[...] = residual
    terms = residual * exch[...].astype(jnp.float32)
    folded = terms[:, :LANES]
    for c in range(1, cols // LANES):
        folded = folded + terms[:, c * LANES:(c + 1) * LANES]
    for q in range(rows // LANES):
        part = folded[q * LANES:(q + 1) * LANES, :].T
        slots[mv, pl.ds(q, 1), :] = jnp.sum(part, axis=0, keepdims=True)

    for s in range(1, nv):
        go(pltpu.make_async_remote_copy(
            src_ref=slots.at[mv], dst_ref=slots.at[mv],
            send_sem=en_send.at[s], recv_sem=en_recv.at[s],
            device_id=(me, lax.rem(mv + s, nv)), device_id_type=MESH,
        ))
    for s in range(1, nv):
        origin = lax.rem(mv + nv - s, nv)
        pltpu.make_async_remote_copy(
            src_ref=slots.at[origin], dst_ref=slots.at[origin],
            send_sem=en_send.at[s], recv_sem=en_recv.at[s],
            device_id=(me, origin), device_id_type=MESH,
        ).wait_recv()
    total = slots[0]
    for v in range(1, nv):
        total = total + slots[v]
    energy_ref[...] = total

    for copy in sent:
        copy.wait_send()


def deliver(residual, energy, residual_out, energy_out, sem):
    copies = [
        pltpu.make_async_copy(residual, residual_out, sem.at[0]),
        pltpu.make_async_copy(energy, energy_out, sem.at[1]),
    ]
    for copy in copies:
        copy.start()
    for copy in copies:
        copy.wait()


def solution(mesh):
    n, nv = mesh.shape["occ"], mesh.shape["virt"]
    chips = n // 2

    def on_device(amplitudes, amp_map, integrals, int_map, exchange, residual_in):
        rows, k = amplitudes.shape
        depth, cols = integrals.shape
        imap = int_map.T
        held = 2 * rows * k + 2 * k * cols + 2 * rows * cols + 8 * rows * cols
        hbm = pl.BlockSpec(memory_space=pltpu.HBM)
        vmem = pl.BlockSpec(memory_space=pltpu.VMEM)
        residual, energy = pl.pallas_call(
            functools.partial(kernel, n, nv),
            out_shape=(
                pltpu.VMEM((rows, cols), jnp.float32),
                pltpu.VMEM((rows // LANES, LANES), jnp.float32),
            ),
            in_specs=[hbm] * 6,
            out_specs=(vmem, vmem),
            scratch_shapes=[
                pltpu.VMEM((rows, k), jnp.bfloat16),
                pltpu.SMEM(amp_map.shape, jnp.int32),
                pltpu.VMEM((k, cols), jnp.bfloat16),
                pltpu.VMEM((2 * depth, cols), jnp.bfloat16),
                pltpu.SMEM(imap.shape, jnp.int32),
                pltpu.VMEM((rows, cols), jnp.bfloat16),
                pltpu.VMEM((rows, cols), jnp.float32),
                pltpu.VMEM((nv, rows // LANES, LANES), jnp.float32),
                pltpu.SemaphoreType.DMA((6,)),
                pltpu.SemaphoreType.DMA((chips, 2)),
                pltpu.SemaphoreType.DMA((chips, 2)),
                pltpu.SemaphoreType.DMA((chips, 2)),
                pltpu.SemaphoreType.DMA((chips, 2)),
                pltpu.SemaphoreType.DMA((nv,)),
                pltpu.SemaphoreType.DMA((nv,)),
            ],
            compiler_params=pltpu.CompilerParams(
                collective_id=0, has_side_effects=True, vmem_limit_bytes=held + (8 << 20)
            ),
            cost_estimate=pl.CostEstimate(flops=2 * rows * k * cols, bytes_accessed=held, transcendentals=0),
        )(*(pltpu.with_memory_space_constraint(x, pltpu.HBM) for x in (amplitudes, amp_map, integrals, imap, exchange, residual_in)))
        residual, energy = pl.pallas_call(
            deliver,
            out_shape=(
                jax.ShapeDtypeStruct((rows, cols), jnp.float32),
                jax.ShapeDtypeStruct((rows // LANES, LANES), jnp.float32),
            ),
            in_specs=[vmem, vmem],
            out_specs=(hbm, hbm),
            scratch_shapes=[pltpu.SemaphoreType.DMA((2,))],
        )(*(pltpu.with_memory_space_constraint(x, pltpu.VMEM) for x in (residual, energy)))
        return residual, energy.reshape(rows)

    in_specs = (
        P("occ", None),
        P("occ", None),
        P("occ", "virt"),
        P(None, "virt"),
        P("occ", "virt"),
        P("occ", "virt"),
    )
    out_specs = (P("occ", "virt"), P("occ"))
    return jax.shard_map(on_device, mesh=mesh, in_specs=in_specs, out_specs=out_specs, check_vma=False)
```

```python
import functools

import jax
import jax.numpy as jnp
from jax import lax
from jax.experimental import pallas as pl
from jax.experimental.pallas import tpu as pltpu
from jax.sharding import PartitionSpec as P

PTILE = 64
VTILE = 128
LANES = 128
PARTS = 1
MESH = pl.DeviceIdType.MESH


def flipped(index, bits):
    out, place = 0, 1
    top = 0
    while place <= bits:
        digit = lax.rem(index // place, 2)
        flip = (bits // place) % 2
        out = out + (1 - digit if flip else digit) * place
        place *= 2
        top = place
    return out + (index // top) * top if top else index


def kernel(
    n, nv,
    amp_hbm, amap_hbm, int_hbm, imap_hbm, exch_hbm, res_hbm,
    out_ref, energy_ref,
    amp, amap, panel, screened, imap, exch, acc, slots,
    in_sem, core_send, core_recv, chip_send, chip_recv, en_send, en_recv,
):
    me = lax.axis_index("occ")
    mv = lax.axis_index("virt")
    chips = n // 2
    chip, core = me // 2, lax.rem(me, 2)
    mate = chip * 2 + (1 - core)
    depth = int_hbm.shape[0]
    rows, cols = out_ref.shape

    def block(owner):
        return panel.at[pl.ds(pl.multiple_of(owner * depth, depth), depth), :]

    loads = [
        pltpu.make_async_copy(int_hbm, block(me), in_sem.at[0]),
        pltpu.make_async_copy(imap_hbm, imap, in_sem.at[1]),
        pltpu.make_async_copy(amp_hbm, amp, in_sem.at[2]),
        pltpu.make_async_copy(amap_hbm, amap, in_sem.at[3]),
        pltpu.make_async_copy(res_hbm, acc, in_sem.at[4]),
        pltpu.make_async_copy(exch_hbm, exch, in_sem.at[5]),
    ]

    partners = [flipped(chip, s) for s in range(chips)]
    barrier = pltpu.get_barrier_semaphore()
    for s in reversed(range(1, chips)):
        pl.semaphore_signal(barrier, inc=1, device_id=(partners[s] * 2 + core, mv), device_id_type=MESH)
    pl.semaphore_signal(barrier, inc=1, device_id=(mate, mv), device_id_type=MESH)
    for s in range(1, nv):
        pl.semaphore_signal(barrier, inc=1, device_id=(me, lax.rem(mv + s, nv)), device_id_type=MESH)
    for load in loads:
        load.start()
    loads[0].wait()
    pl.semaphore_wait(barrier, chips + nv - 1)

    def push(owner, target, send, recv):
        return pltpu.make_async_remote_copy(
            src_ref=block(owner), dst_ref=block(owner),
            send_sem=send, recv_sem=recv, device_id=(target, mv), device_id_type=MESH,
        )

    theirs = [p * 2 + core for p in partners]
    theirs[0] = me
    others = [p * 2 + (1 - core) for p in partners]

    def to_mate(s):
        return push(theirs[s], mate, core_send.at[s], core_recv.at[s])

    def from_mate(s):
        return push(others[s], mate, core_send.at[s], core_recv.at[s])

    def to_chip(s):
        return push(me, theirs[s], chip_send.at[s], chip_recv.at[s])

    def from_chip(s):
        return push(theirs[s], theirs[s], chip_send.at[s], chip_recv.at[s])

    sent = []

    def go(copy):
        copy.start()
        sent.append(copy)

    for s in range(1, chips):
        go(to_chip(s))
    go(to_mate(0))

    loads[2].wait()
    loads[3].wait()
    for r in range(rows // PTILE):
        tall = pl.ds(r * PTILE, PTILE)
        for k in range(amp.shape[1] // VTILE):
            wide = pl.ds(k * VTILE, VTILE)
            keep = amap[r, k].astype(jnp.float32).astype(jnp.bfloat16)
            amp[tall, wide] = amp[tall, wide] * keep
    loads[4].wait()
    loads[5].wait()
    loads[1].wait()
    span = 2 * depth
    grain = min(span, VTILE)
    while span % grain or VTILE % grain:
        grain //= 2

    def product(s):
        start = partners[s] * span
        for t in range(span // grain):
            tile = (start + t * grain) // VTILE
            here = pl.ds(pl.multiple_of(start + t * grain, grain), grain)
            for c in range(cols // VTILE):
                wide = pl.ds(c * VTILE, VTILE)
                keep = imap[c, tile].astype(jnp.float32).astype(jnp.bfloat16)
                screened[pl.ds(t * grain, grain), wide] = panel[here, wide] * keep
        return jnp.dot(
            amp[:, pl.ds(pl.multiple_of(start, LANES), span)], screened[...],
            preferred_element_type=jnp.float32,
        )

    for s in range(1, chips):
        if s == chips - 1:
            from_mate(0).wait_recv()
            acc[...] += product(0)
        from_chip(s).wait_recv()
        go(to_mate(s))
    for s in range(1, chips):
        from_mate(s).wait_recv()
        if s < chips - 1:
            acc[...] += product(s)

    residual = acc[...] + product(chips - 1)
    out_ref[...] = residual
    terms = residual * exch[...].astype(jnp.float32)
    folded = terms[:, :LANES]
    for c in range(1, cols // LANES):
        folded = folded + terms[:, c * LANES:(c + 1) * LANES]
    for q in range(rows // LANES):
        part = folded[q * LANES:(q + 1) * LANES, :].T
        slots[mv, pl.ds(q, 1), :] = jnp.sum(part, axis=0, keepdims=True)

    for s in range(1, nv):
        go(pltpu.make_async_remote_copy(
            src_ref=slots.at[mv], dst_ref=slots.at[mv],
            send_sem=en_send.at[s], recv_sem=en_recv.at[s],
            device_id=(me, lax.rem(mv + s, nv)), device_id_type=MESH,
        ))
    for s in range(1, nv):
        origin = lax.rem(mv + nv - s, nv)
        pltpu.make_async_remote_copy(
            src_ref=slots.at[origin], dst_ref=slots.at[origin],
            send_sem=en_send.at[s], recv_sem=en_recv.at[s],
            device_id=(me, origin), device_id_type=MESH,
        ).wait_recv()
    total = slots[0]
    for v in range(1, nv):
        total = total + slots[v]
    energy_ref[...] = total

    for copy in sent:
        copy.wait_send()


def deliver(residual, energy, residual_out, energy_out, sem):
    part = residual.shape[0] // PARTS
    copies = [pltpu.make_async_copy(energy, energy_out, sem.at[PARTS])]
    for p in range(PARTS):
        here = pl.ds(p * part, part)
        copies.append(pltpu.make_async_copy(residual.at[here, :], residual_out.at[here, :], sem.at[p]))
    for copy in copies:
        copy.start()
    for copy in copies:
        copy.wait()


def solution(mesh):
    n, nv = mesh.shape["occ"], mesh.shape["virt"]
    chips = n // 2

    def on_device(amplitudes, amp_map, integrals, int_map, exchange, residual_in):
        rows, k = amplitudes.shape
        depth, cols = integrals.shape
        imap = int_map.T
        held = 2 * rows * k + 2 * k * cols + 2 * rows * cols + 8 * rows * cols
        hbm = pl.BlockSpec(memory_space=pltpu.HBM)
        vmem = pl.BlockSpec(memory_space=pltpu.VMEM)
        residual, energy = pl.pallas_call(
            functools.partial(kernel, n, nv),
            out_shape=(
                pltpu.VMEM((rows, cols), jnp.float32),
                pltpu.VMEM((rows // LANES, LANES), jnp.float32),
            ),
            in_specs=[hbm] * 6,
            out_specs=(vmem, vmem),
            scratch_shapes=[
                pltpu.VMEM((rows, k), jnp.bfloat16),
                pltpu.SMEM(amp_map.shape, jnp.int32),
                pltpu.VMEM((k, cols), jnp.bfloat16),
                pltpu.VMEM((2 * depth, cols), jnp.bfloat16),
                pltpu.SMEM(imap.shape, jnp.int32),
                pltpu.VMEM((rows, cols), jnp.bfloat16),
                pltpu.VMEM((rows, cols), jnp.float32),
                pltpu.VMEM((nv, rows // LANES, LANES), jnp.float32),
                pltpu.SemaphoreType.DMA((6,)),
                pltpu.SemaphoreType.DMA((chips,)),
                pltpu.SemaphoreType.DMA((chips,)),
                pltpu.SemaphoreType.DMA((chips,)),
                pltpu.SemaphoreType.DMA((chips,)),
                pltpu.SemaphoreType.DMA((nv,)),
                pltpu.SemaphoreType.DMA((nv,)),
            ],
            compiler_params=pltpu.CompilerParams(
                collective_id=0, has_side_effects=True, vmem_limit_bytes=held + (8 << 20)
            ),
            cost_estimate=pl.CostEstimate(flops=2 * rows * k * cols, bytes_accessed=held, transcendentals=0),
        )(*(pltpu.with_memory_space_constraint(x, pltpu.HBM) for x in (amplitudes, amp_map, integrals, imap, exchange, residual_in)))
        residual, energy = pl.pallas_call(
            deliver,
            out_shape=(
                jax.ShapeDtypeStruct((rows, cols), jnp.float32),
                jax.ShapeDtypeStruct((rows // LANES, LANES), jnp.float32),
            ),
            in_specs=[vmem, vmem],
            out_specs=(hbm, hbm),
            scratch_shapes=[pltpu.SemaphoreType.DMA((PARTS + 1,))],
        )(*(pltpu.with_memory_space_constraint(x, pltpu.VMEM) for x in (residual, energy)))
        return residual, energy.reshape(rows)

    in_specs = (
        P("occ", None),
        P("occ", None),
        P("occ", "virt"),
        P(None, "virt"),
        P("occ", "virt"),
        P("occ", "virt"),
    )
    out_specs = (P("occ", "virt"), P("occ"))
    return jax.shard_map(on_device, mesh=mesh, in_specs=in_specs, out_specs=out_specs, check_vma=False)
```

```python
import functools

import jax
import jax.numpy as jnp
from jax import lax
from jax.experimental import pallas as pl
from jax.experimental.pallas import tpu as pltpu
from jax.sharding import PartitionSpec as P

PTILE = 64
VTILE = 128
LANES = 128
PARTS = 1
MESH = pl.DeviceIdType.MESH


def flipped(index, bits):
    out, place = 0, 1
    top = 0
    while place <= bits:
        digit = lax.rem(index // place, 2)
        flip = (bits // place) % 2
        out = out + (1 - digit if flip else digit) * place
        place *= 2
        top = place
    return out + (index // top) * top if top else index


def kernel(
    n, nv,
    amp_hbm, amap_hbm, int_hbm, imap_hbm, exch_hbm, res_hbm,
    out_ref, energy_ref,
    amp, amap, panel, screened, imap, exch, acc, slots,
    in_sem, core_send, core_recv, chip_send, chip_recv, en_send, en_recv,
):
    me = lax.axis_index("occ")
    mv = lax.axis_index("virt")
    chips = n // 2
    chip, core = me // 2, lax.rem(me, 2)
    mate = chip * 2 + (1 - core)
    depth = int_hbm.shape[0]
    rows, cols = out_ref.shape

    def block(owner):
        return panel.at[pl.ds(pl.multiple_of(owner * depth, depth), depth), :]

    loads = [
        pltpu.make_async_copy(int_hbm, block(me), in_sem.at[0]),
        pltpu.make_async_copy(imap_hbm, imap, in_sem.at[1]),
        pltpu.make_async_copy(amp_hbm, amp, in_sem.at[2]),
        pltpu.make_async_copy(amap_hbm, amap, in_sem.at[3]),
        pltpu.make_async_copy(res_hbm, acc, in_sem.at[4]),
        pltpu.make_async_copy(exch_hbm, exch, in_sem.at[5]),
    ]

    partners = [flipped(chip, s) for s in range(chips)]
    barrier = pltpu.get_barrier_semaphore()
    for s in reversed(range(1, chips)):
        pl.semaphore_signal(barrier, inc=1, device_id=(partners[s] * 2 + core, mv), device_id_type=MESH)
    pl.semaphore_signal(barrier, inc=1, device_id=(mate, mv), device_id_type=MESH)
    for s in range(1, nv):
        pl.semaphore_signal(barrier, inc=1, device_id=(me, lax.rem(mv + s, nv)), device_id_type=MESH)
    for load in loads:
        load.start()
    loads[0].wait()
    pl.semaphore_wait(barrier, chips + nv - 1)

    def push(owner, target, send, recv):
        return pltpu.make_async_remote_copy(
            src_ref=block(owner), dst_ref=block(owner),
            send_sem=send, recv_sem=recv, device_id=(target, mv), device_id_type=MESH,
        )

    theirs = [p * 2 + core for p in partners]
    theirs[0] = me
    others = [p * 2 + (1 - core) for p in partners]

    def to_mate(s):
        return push(theirs[s], mate, core_send.at[s], core_recv.at[s])

    def from_mate(s):
        return push(others[s], mate, core_send.at[s], core_recv.at[s])

    def to_chip(s):
        return push(me, theirs[s], chip_send.at[s], chip_recv.at[s])

    def from_chip(s):
        return push(theirs[s], theirs[s], chip_send.at[s], chip_recv.at[s])

    sent = []

    def go(copy):
        copy.start()
        sent.append(copy)

    for s in reversed(range(1, chips)):
        go(to_chip(s))
    go(to_mate(0))

    span = 2 * depth
    grain = min(span, VTILE)
    while span % grain or VTILE % grain:
        grain //= 2

    def product(s):
        start = partners[s] * span
        for t in range(span // grain):
            tile = (start + t * grain) // VTILE
            here = pl.ds(pl.multiple_of(start + t * grain, grain), grain)
            for c in range(cols // VTILE):
                wide = pl.ds(c * VTILE, VTILE)
                keep = imap[c, tile].astype(jnp.float32).astype(jnp.bfloat16)
                screened[pl.ds(t * grain, grain), wide] = panel[here, wide] * keep
        return jnp.dot(
            amp[:, pl.ds(pl.multiple_of(start, LANES), span)], screened[...],
            preferred_element_type=jnp.float32,
        )

    for s in range(1, chips):
        from_chip(s).wait_recv()
        go(to_mate(s))

    loads[2].wait()
    loads[3].wait()
    for r in range(rows // PTILE):
        tall = pl.ds(r * PTILE, PTILE)
        for k in range(amp.shape[1] // VTILE):
            wide = pl.ds(k * VTILE, VTILE)
            keep = amap[r, k].astype(jnp.float32).astype(jnp.bfloat16)
            amp[tall, wide] = amp[tall, wide] * keep
    loads[4].wait()
    loads[5].wait()
    loads[1].wait()
    for s in range(chips):
        from_mate(s).wait_recv()
        if s < chips - 1:
            acc[...] += product(s)

    residual = acc[...] + product(chips - 1)
    out_ref[...] = residual
    terms = residual * exch[...].astype(jnp.float32)
    folded = terms[:, :LANES]
    for c in range(1, cols // LANES):
        folded = folded + terms[:, c * LANES:(c + 1) * LANES]
    for q in range(rows // LANES):
        part = folded[q * LANES:(q + 1) * LANES, :].T
        slots[mv, pl.ds(q, 1), :] = jnp.sum(part, axis=0, keepdims=True)

    for s in range(1, nv):
        go(pltpu.make_async_remote_copy(
            src_ref=slots.at[mv], dst_ref=slots.at[mv],
            send_sem=en_send.at[s], recv_sem=en_recv.at[s],
            device_id=(me, lax.rem(mv + s, nv)), device_id_type=MESH,
        ))
    for s in range(1, nv):
        origin = lax.rem(mv + nv - s, nv)
        pltpu.make_async_remote_copy(
            src_ref=slots.at[origin], dst_ref=slots.at[origin],
            send_sem=en_send.at[s], recv_sem=en_recv.at[s],
            device_id=(me, origin), device_id_type=MESH,
        ).wait_recv()
    total = slots[0]
    for v in range(1, nv):
        total = total + slots[v]
    energy_ref[...] = total

    for copy in sent:
        copy.wait_send()


def deliver(residual, energy, residual_out, energy_out, sem):
    part = residual.shape[0] // PARTS
    copies = [pltpu.make_async_copy(energy, energy_out, sem.at[PARTS])]
    for p in range(PARTS):
        here = pl.ds(p * part, part)
        copies.append(pltpu.make_async_copy(residual.at[here, :], residual_out.at[here, :], sem.at[p]))
    for copy in copies:
        copy.start()
    for copy in copies:
        copy.wait()


def solution(mesh):
    n, nv = mesh.shape["occ"], mesh.shape["virt"]
    chips = n // 2

    def on_device(amplitudes, amp_map, integrals, int_map, exchange, residual_in):
        rows, k = amplitudes.shape
        depth, cols = integrals.shape
        imap = int_map.T
        held = 2 * rows * k + 2 * k * cols + 2 * rows * cols + 8 * rows * cols
        hbm = pl.BlockSpec(memory_space=pltpu.HBM)
        vmem = pl.BlockSpec(memory_space=pltpu.VMEM)
        residual, energy = pl.pallas_call(
            functools.partial(kernel, n, nv),
            out_shape=(
                pltpu.VMEM((rows, cols), jnp.float32),
                pltpu.VMEM((rows // LANES, LANES), jnp.float32),
            ),
            in_specs=[hbm] * 6,
            out_specs=(vmem, vmem),
            scratch_shapes=[
                pltpu.VMEM((rows, k), jnp.bfloat16),
                pltpu.SMEM(amp_map.shape, jnp.int32),
                pltpu.VMEM((k, cols), jnp.bfloat16),
                pltpu.VMEM((2 * depth, cols), jnp.bfloat16),
                pltpu.SMEM(imap.shape, jnp.int32),
                pltpu.VMEM((rows, cols), jnp.bfloat16),
                pltpu.VMEM((rows, cols), jnp.float32),
                pltpu.VMEM((nv, rows // LANES, LANES), jnp.float32),
                pltpu.SemaphoreType.DMA((6,)),
                pltpu.SemaphoreType.DMA((chips,)),
                pltpu.SemaphoreType.DMA((chips,)),
                pltpu.SemaphoreType.DMA((chips,)),
                pltpu.SemaphoreType.DMA((chips,)),
                pltpu.SemaphoreType.DMA((nv,)),
                pltpu.SemaphoreType.DMA((nv,)),
            ],
            compiler_params=pltpu.CompilerParams(
                collective_id=0, has_side_effects=True, vmem_limit_bytes=held + (8 << 20)
            ),
            cost_estimate=pl.CostEstimate(flops=2 * rows * k * cols, bytes_accessed=held, transcendentals=0),
        )(*(pltpu.with_memory_space_constraint(x, pltpu.HBM) for x in (amplitudes, amp_map, integrals, imap, exchange, residual_in)))
        residual, energy = pl.pallas_call(
            deliver,
            out_shape=(
                jax.ShapeDtypeStruct((rows, cols), jnp.float32),
                jax.ShapeDtypeStruct((rows // LANES, LANES), jnp.float32),
            ),
            in_specs=[vmem, vmem],
            out_specs=(hbm, hbm),
            scratch_shapes=[pltpu.SemaphoreType.DMA((PARTS + 1,))],
        )(*(pltpu.with_memory_space_constraint(x, pltpu.VMEM) for x in (residual, energy)))
        return residual, energy.reshape(rows)

    in_specs = (
        P("occ", None),
        P("occ", None),
        P("occ", "virt"),
        P(None, "virt"),
        P("occ", "virt"),
        P("occ", "virt"),
    )
    out_specs = (P("occ", "virt"), P("occ"))
    return jax.shard_map(on_device, mesh=mesh, in_specs=in_specs, out_specs=out_specs, check_vma=False)
```

```python
import functools

import jax
import jax.numpy as jnp
from jax import lax
from jax.experimental import pallas as pl
from jax.experimental.pallas import tpu as pltpu
from jax.sharding import PartitionSpec as P

PTILE = 64
VTILE = 128
LANES = 128
PARTS = 1
MESH = pl.DeviceIdType.MESH


def flipped(index, bits):
    out, place = 0, 1
    top = 0
    while place <= bits:
        digit = lax.rem(index // place, 2)
        flip = (bits // place) % 2
        out = out + (1 - digit if flip else digit) * place
        place *= 2
        top = place
    return out + (index // top) * top if top else index


def kernel(
    n, nv,
    amp_hbm, amap_hbm, int_hbm, imap_hbm, exch_hbm, res_hbm,
    out_ref, energy_ref,
    amp, amap, panel, screened, imap, exch, acc, slots,
    in_sem, core_send, core_recv, chip_send, chip_recv, en_send, en_recv,
):
    me = lax.axis_index("occ")
    mv = lax.axis_index("virt")
    chips = n // 2
    chip, core = me // 2, lax.rem(me, 2)
    mate = chip * 2 + (1 - core)
    depth = int_hbm.shape[0]
    rows, cols = out_ref.shape

    def block(owner):
        return panel.at[pl.ds(pl.multiple_of(owner * depth, depth), depth), :]

    loads = [
        pltpu.make_async_copy(int_hbm, block(me), in_sem.at[0]),
        pltpu.make_async_copy(imap_hbm, imap, in_sem.at[1]),
        pltpu.make_async_copy(amp_hbm, amp, in_sem.at[2]),
        pltpu.make_async_copy(amap_hbm, amap, in_sem.at[3]),
        pltpu.make_async_copy(res_hbm, acc, in_sem.at[4]),
        pltpu.make_async_copy(exch_hbm, exch, in_sem.at[5]),
    ]

    partners = [flipped(chip, s) for s in range(chips)]
    barrier = pltpu.get_barrier_semaphore()
    for s in reversed(range(1, chips)):
        pl.semaphore_signal(barrier, inc=1, device_id=(partners[s] * 2 + core, mv), device_id_type=MESH)
    pl.semaphore_signal(barrier, inc=1, device_id=(mate, mv), device_id_type=MESH)
    for s in range(1, nv):
        pl.semaphore_signal(barrier, inc=1, device_id=(me, lax.rem(mv + s, nv)), device_id_type=MESH)
    for load in loads:
        load.start()
    loads[0].wait()
    pl.semaphore_wait(barrier, chips + nv - 1)

    def push(owner, target, send, recv):
        return pltpu.make_async_remote_copy(
            src_ref=block(owner), dst_ref=block(owner),
            send_sem=send, recv_sem=recv, device_id=(target, mv), device_id_type=MESH,
        )

    theirs = [p * 2 + core for p in partners]
    theirs[0] = me
    others = [p * 2 + (1 - core) for p in partners]

    def to_mate(s):
        return push(theirs[s], mate, core_send.at[s], core_recv.at[s])

    def from_mate(s):
        return push(others[s], mate, core_send.at[s], core_recv.at[s])

    def to_chip(s):
        return push(me, theirs[s], chip_send.at[s], chip_recv.at[s])

    def from_chip(s):
        return push(theirs[s], theirs[s], chip_send.at[s], chip_recv.at[s])

    sent = []

    def go(copy):
        copy.start()
        sent.append(copy)

    for s in reversed(range(1, chips)):
        go(to_chip(s))
    go(to_mate(0))

    loads[2].wait()
    loads[3].wait()
    for r in range(rows // PTILE):
        tall = pl.ds(r * PTILE, PTILE)
        for k in range(amp.shape[1] // VTILE):
            wide = pl.ds(k * VTILE, VTILE)
            keep = amap[r, k].astype(jnp.float32).astype(jnp.bfloat16)
            amp[tall, wide] = amp[tall, wide] * keep
    loads[4].wait()
    loads[5].wait()
    loads[1].wait()
    span = 2 * depth
    grain = min(span, VTILE)
    while span % grain or VTILE % grain:
        grain //= 2

    def product(s):
        start = partners[s] * span
        for t in range(span // grain):
            tile = (start + t * grain) // VTILE
            here = pl.ds(pl.multiple_of(start + t * grain, grain), grain)
            for c in range(cols // VTILE):
                wide = pl.ds(c * VTILE, VTILE)
                keep = imap[c, tile].astype(jnp.float32).astype(jnp.bfloat16)
                screened[pl.ds(t * grain, grain), wide] = panel[here, wide] * keep
        return jnp.dot(
            amp[:, pl.ds(pl.multiple_of(start, LANES), span)], screened[...],
            preferred_element_type=jnp.float32,
        )

    from_mate(0).wait_recv()
    if chips > 1:
        acc[...] += product(0)
    for s in range(1, chips):
        from_chip(s).wait_recv()
        go(to_mate(s))
    for s in range(1, chips):
        from_mate(s).wait_recv()
        if s < chips - 1:
            acc[...] += product(s)

    residual = acc[...] + product(chips - 1)
    out_ref[...] = residual
    terms = residual * exch[...].astype(jnp.float32)
    folded = terms[:, :LANES]
    for c in range(1, cols // LANES):
        folded = folded + terms[:, c * LANES:(c + 1) * LANES]
    for q in range(rows // LANES):
        part = folded[q * LANES:(q + 1) * LANES, :].T
        slots[mv, pl.ds(q, 1), :] = jnp.sum(part, axis=0, keepdims=True)

    for s in range(1, nv):
        go(pltpu.make_async_remote_copy(
            src_ref=slots.at[mv], dst_ref=slots.at[mv],
            send_sem=en_send.at[s], recv_sem=en_recv.at[s],
            device_id=(me, lax.rem(mv + s, nv)), device_id_type=MESH,
        ))
    for s in range(1, nv):
        origin = lax.rem(mv + nv - s, nv)
        pltpu.make_async_remote_copy(
            src_ref=slots.at[origin], dst_ref=slots.at[origin],
            send_sem=en_send.at[s], recv_sem=en_recv.at[s],
            device_id=(me, origin), device_id_type=MESH,
        ).wait_recv()
    total = slots[0]
    for v in range(1, nv):
        total = total + slots[v]
    energy_ref[...] = total

    for copy in sent:
        copy.wait_send()


def deliver(residual, energy, residual_out, energy_out, sem):
    part = residual.shape[0] // PARTS
    copies = [pltpu.make_async_copy(energy, energy_out, sem.at[PARTS])]
    for p in range(PARTS):
        here = pl.ds(p * part, part)
        copies.append(pltpu.make_async_copy(residual.at[here, :], residual_out.at[here, :], sem.at[p]))
    for copy in copies:
        copy.start()
    for copy in copies:
        copy.wait()


def solution(mesh):
    n, nv = mesh.shape["occ"], mesh.shape["virt"]
    chips = n // 2

    def on_device(amplitudes, amp_map, integrals, int_map, exchange, residual_in):
        rows, k = amplitudes.shape
        depth, cols = integrals.shape
        imap = int_map.T
        held = 2 * rows * k + 2 * k * cols + 2 * rows * cols + 8 * rows * cols
        hbm = pl.BlockSpec(memory_space=pltpu.HBM)
        vmem = pl.BlockSpec(memory_space=pltpu.VMEM)
        residual, energy = pl.pallas_call(
            functools.partial(kernel, n, nv),
            out_shape=(
                pltpu.VMEM((rows, cols), jnp.float32),
                pltpu.VMEM((rows // LANES, LANES), jnp.float32),
            ),
            in_specs=[hbm] * 6,
            out_specs=(vmem, vmem),
            scratch_shapes=[
                pltpu.VMEM((rows, k), jnp.bfloat16),
                pltpu.SMEM(amp_map.shape, jnp.int32),
                pltpu.VMEM((k, cols), jnp.bfloat16),
                pltpu.VMEM((2 * depth, cols), jnp.bfloat16),
                pltpu.SMEM(imap.shape, jnp.int32),
                pltpu.VMEM((rows, cols), jnp.bfloat16),
                pltpu.VMEM((rows, cols), jnp.float32),
                pltpu.VMEM((nv, rows // LANES, LANES), jnp.float32),
                pltpu.SemaphoreType.DMA((6,)),
                pltpu.SemaphoreType.DMA((chips,)),
                pltpu.SemaphoreType.DMA((chips,)),
                pltpu.SemaphoreType.DMA((chips,)),
                pltpu.SemaphoreType.DMA((chips,)),
                pltpu.SemaphoreType.DMA((nv,)),
                pltpu.SemaphoreType.DMA((nv,)),
            ],
            compiler_params=pltpu.CompilerParams(
                collective_id=0, has_side_effects=True, vmem_limit_bytes=held + (8 << 20)
            ),
            cost_estimate=pl.CostEstimate(flops=2 * rows * k * cols, bytes_accessed=held, transcendentals=0),
        )(*(pltpu.with_memory_space_constraint(x, pltpu.HBM) for x in (amplitudes, amp_map, integrals, imap, exchange, residual_in)))
        residual, energy = pl.pallas_call(
            deliver,
            out_shape=(
                jax.ShapeDtypeStruct((rows, cols), jnp.float32),
                jax.ShapeDtypeStruct((rows // LANES, LANES), jnp.float32),
            ),
            in_specs=[vmem, vmem],
            out_specs=(hbm, hbm),
            scratch_shapes=[pltpu.SemaphoreType.DMA((PARTS + 1,))],
        )(*(pltpu.with_memory_space_constraint(x, pltpu.VMEM) for x in (residual, energy)))
        return residual, energy.reshape(rows)

    in_specs = (
        P("occ", None),
        P("occ", None),
        P("occ", "virt"),
        P(None, "virt"),
        P("occ", "virt"),
        P("occ", "virt"),
    )
    out_specs = (P("occ", "virt"), P("occ"))
    return jax.shard_map(on_device, mesh=mesh, in_specs=in_specs, out_specs=out_specs, check_vma=False)
```

```python
import functools

import jax
import jax.numpy as jnp
from jax import lax
from jax.experimental import pallas as pl
from jax.experimental.pallas import tpu as pltpu
from jax.sharding import PartitionSpec as P

PTILE = 64
VTILE = 128
LANES = 128
PARTS = 1
MESH = pl.DeviceIdType.MESH


def flipped(index, bits):
    out, place = 0, 1
    top = 0
    while place <= bits:
        digit = lax.rem(index // place, 2)
        flip = (bits // place) % 2
        out = out + (1 - digit if flip else digit) * place
        place *= 2
        top = place
    return out + (index // top) * top if top else index


def kernel(
    n, nv,
    amp_hbm, amap_hbm, int_hbm, imap_hbm, exch_hbm, res_hbm,
    out_ref, energy_ref,
    amp, amap, panel, screened, imap, exch, acc, slots,
    in_sem, core_send, core_recv, chip_send, chip_recv, en_send, en_recv,
):
    me = lax.axis_index("occ")
    mv = lax.axis_index("virt")
    chips = n // 2
    chip, core = me // 2, lax.rem(me, 2)
    mate = chip * 2 + (1 - core)
    depth = int_hbm.shape[0]
    rows, cols = out_ref.shape

    def block(owner):
        return panel.at[pl.ds(pl.multiple_of(owner * depth, depth), depth), :]

    loads = [
        pltpu.make_async_copy(int_hbm, block(me), in_sem.at[0]),
        pltpu.make_async_copy(imap_hbm, imap, in_sem.at[1]),
        pltpu.make_async_copy(amp_hbm, amp, in_sem.at[2]),
        pltpu.make_async_copy(amap_hbm, amap, in_sem.at[3]),
        pltpu.make_async_copy(res_hbm, acc, in_sem.at[4]),
        pltpu.make_async_copy(exch_hbm, exch, in_sem.at[5]),
    ]

    partners = [flipped(chip, s) for s in range(chips)]
    barrier = pltpu.get_barrier_semaphore()
    for s in reversed(range(1, chips)):
        pl.semaphore_signal(barrier, inc=1, device_id=(partners[s] * 2 + core, mv), device_id_type=MESH)
    pl.semaphore_signal(barrier, inc=1, device_id=(mate, mv), device_id_type=MESH)
    for s in range(1, nv):
        pl.semaphore_signal(barrier, inc=1, device_id=(me, lax.rem(mv + s, nv)), device_id_type=MESH)
    for load in loads:
        load.start()
    loads[0].wait()
    pl.semaphore_wait(barrier, chips + nv - 1)

    def push(owner, target, send, recv):
        return pltpu.make_async_remote_copy(
            src_ref=block(owner), dst_ref=block(owner),
            send_sem=send, recv_sem=recv, device_id=(target, mv), device_id_type=MESH,
        )

    theirs = [p * 2 + core for p in partners]
    theirs[0] = me
    others = [p * 2 + (1 - core) for p in partners]

    def to_mate(s):
        return push(theirs[s], mate, core_send.at[s], core_recv.at[s])

    def from_mate(s):
        return push(others[s], mate, core_send.at[s], core_recv.at[s])

    def to_chip(s):
        return push(me, theirs[s], chip_send.at[s], chip_recv.at[s])

    def from_chip(s):
        return push(theirs[s], theirs[s], chip_send.at[s], chip_recv.at[s])

    sent = []

    def go(copy):
        copy.start()
        sent.append(copy)

    for s in reversed(range(1, chips)):
        go(to_chip(s))
    go(to_mate(0))

    loads[2].wait()
    loads[3].wait()
    for r in range(rows // PTILE):
        tall = pl.ds(r * PTILE, PTILE)
        for k in range(amp.shape[1] // VTILE):
            wide = pl.ds(k * VTILE, VTILE)
            keep = amap[r, k].astype(jnp.float32).astype(jnp.bfloat16)
            amp[tall, wide] = amp[tall, wide] * keep
    loads[4].wait()
    loads[5].wait()
    loads[1].wait()
    span = 2 * depth
    grain = min(span, VTILE)
    while span % grain or VTILE % grain:
        grain //= 2

    def product(s):
        start = partners[s] * span
        for t in range(span // grain):
            tile = (start + t * grain) // VTILE
            here = pl.ds(pl.multiple_of(start + t * grain, grain), grain)
            for c in range(cols // VTILE):
                wide = pl.ds(c * VTILE, VTILE)
                keep = imap[c, tile].astype(jnp.float32).astype(jnp.bfloat16)
                screened[pl.ds(t * grain, grain), wide] = panel[here, wide] * keep
        return jnp.dot(
            amp[:, pl.ds(pl.multiple_of(start, LANES), span)], screened[...],
            preferred_element_type=jnp.float32,
        )

    from_mate(0).wait_recv()
    if chips > 1:
        acc[...] += product(0)
    for s in reversed(range(1, chips)):
        from_chip(s).wait_recv()
        go(to_mate(s))
    for s in reversed(range(1, chips)):
        from_mate(s).wait_recv()
        if s > 1:
            acc[...] += product(s)

    residual = acc[...] + product(min(1, chips - 1))
    out_ref[...] = residual
    terms = residual * exch[...].astype(jnp.float32)
    folded = terms[:, :LANES]
    for c in range(1, cols // LANES):
        folded = folded + terms[:, c * LANES:(c + 1) * LANES]
    for q in range(rows // LANES):
        part = folded[q * LANES:(q + 1) * LANES, :].T
        slots[mv, pl.ds(q, 1), :] = jnp.sum(part, axis=0, keepdims=True)

    for s in range(1, nv):
        go(pltpu.make_async_remote_copy(
            src_ref=slots.at[mv], dst_ref=slots.at[mv],
            send_sem=en_send.at[s], recv_sem=en_recv.at[s],
            device_id=(me, lax.rem(mv + s, nv)), device_id_type=MESH,
        ))
    for s in range(1, nv):
        origin = lax.rem(mv + nv - s, nv)
        pltpu.make_async_remote_copy(
            src_ref=slots.at[origin], dst_ref=slots.at[origin],
            send_sem=en_send.at[s], recv_sem=en_recv.at[s],
            device_id=(me, origin), device_id_type=MESH,
        ).wait_recv()
    total = slots[0]
    for v in range(1, nv):
        total = total + slots[v]
    energy_ref[...] = total

    for copy in sent:
        copy.wait_send()


def deliver(residual, energy, residual_out, energy_out, sem):
    part = residual.shape[0] // PARTS
    copies = [pltpu.make_async_copy(energy, energy_out, sem.at[PARTS])]
    for p in range(PARTS):
        here = pl.ds(p * part, part)
        copies.append(pltpu.make_async_copy(residual.at[here, :], residual_out.at[here, :], sem.at[p]))
    for copy in copies:
        copy.start()
    for copy in copies:
        copy.wait()


def solution(mesh):
    n, nv = mesh.shape["occ"], mesh.shape["virt"]
    chips = n // 2

    def on_device(amplitudes, amp_map, integrals, int_map, exchange, residual_in):
        rows, k = amplitudes.shape
        depth, cols = integrals.shape
        imap = int_map.T
        held = 2 * rows * k + 2 * k * cols + 2 * rows * cols + 8 * rows * cols
        hbm = pl.BlockSpec(memory_space=pltpu.HBM)
        vmem = pl.BlockSpec(memory_space=pltpu.VMEM)
        residual, energy = pl.pallas_call(
            functools.partial(kernel, n, nv),
            out_shape=(
                pltpu.VMEM((rows, cols), jnp.float32),
                pltpu.VMEM((rows // LANES, LANES), jnp.float32),
            ),
            in_specs=[hbm] * 6,
            out_specs=(vmem, vmem),
            scratch_shapes=[
                pltpu.VMEM((rows, k), jnp.bfloat16),
                pltpu.SMEM(amp_map.shape, jnp.int32),
                pltpu.VMEM((k, cols), jnp.bfloat16),
                pltpu.VMEM((2 * depth, cols), jnp.bfloat16),
                pltpu.SMEM(imap.shape, jnp.int32),
                pltpu.VMEM((rows, cols), jnp.bfloat16),
                pltpu.VMEM((rows, cols), jnp.float32),
                pltpu.VMEM((nv, rows // LANES, LANES), jnp.float32),
                pltpu.SemaphoreType.DMA((6,)),
                pltpu.SemaphoreType.DMA((chips,)),
                pltpu.SemaphoreType.DMA((chips,)),
                pltpu.SemaphoreType.DMA((chips,)),
                pltpu.SemaphoreType.DMA((chips,)),
                pltpu.SemaphoreType.DMA((nv,)),
                pltpu.SemaphoreType.DMA((nv,)),
            ],
            compiler_params=pltpu.CompilerParams(
                collective_id=0, has_side_effects=True, vmem_limit_bytes=held + (8 << 20)
            ),
            cost_estimate=pl.CostEstimate(flops=2 * rows * k * cols, bytes_accessed=held, transcendentals=0),
        )(*(pltpu.with_memory_space_constraint(x, pltpu.HBM) for x in (amplitudes, amp_map, integrals, imap, exchange, residual_in)))
        residual, energy = pl.pallas_call(
            deliver,
            out_shape=(
                jax.ShapeDtypeStruct((rows, cols), jnp.float32),
                jax.ShapeDtypeStruct((rows // LANES, LANES), jnp.float32),
            ),
            in_specs=[vmem, vmem],
            out_specs=(hbm, hbm),
            scratch_shapes=[pltpu.SemaphoreType.DMA((PARTS + 1,))],
        )(*(pltpu.with_memory_space_constraint(x, pltpu.VMEM) for x in (residual, energy)))
        return residual, energy.reshape(rows)

    in_specs = (
        P("occ", None),
        P("occ", None),
        P("occ", "virt"),
        P(None, "virt"),
        P("occ", "virt"),
        P("occ", "virt"),
    )
    out_specs = (P("occ", "virt"), P("occ"))
    return jax.shard_map(on_device, mesh=mesh, in_specs=in_specs, out_specs=out_specs, check_vma=False)
```
